128 devices in a mesh: wide: 16 (over x, y), narrow: 8 (over z, core).
Axes of the slice: x: 4, y: 4, z: 4, core: 2. Of those that a mesh axis runs over, the one named last changes fastest.
Arguments:
- potential: float32 [8, 256, 256, 128], P(None, 'wide', 'narrow'), may hold values from -6 to 6
- source_current: float32 [3, 256, 256, 128], P(None, 'wide', 'narrow'), may hold values from -6 to 6
- cell_label: int32 [256, 256, 128], P('wide', 'narrow'), may hold values from 0 to 47
- region_kappa: float32 [16], replicated, may hold values from 0.5 to 4
- send_lines: int32 [128, 128, 4], P(('wide', 'narrow')), may hold values from 0 to 511, as said below
- recv_slot: int32 [128, 256], P(('wide', 'narrow')), may hold values from 0 to 511, as said below
- velocity: float32 [3, 128, 256, 128], P(None, 'wide', 'narrow'), may hold values from -6 to 6
Outputs:
- potential_next: float32 [8, 256, 256, 128], P(None, 'wide', 'narrow')
- les_force: bfloat16 [3, 128, 256, 128], P(None, 'wide', 'narrow')
- velocity_next: float32 [3, 128, 256, 128], P(None, 'wide', 'narrow')
The draws below stay inside these ranges and needn't reach their ends.
Inputs may be any that keep to these rules, and one draw needn't show every extreme that they name: send_lines[e, l, c] is a line of device e's EM block; over the pairs that recv_slot uses, each line of device e is named at most once. `recv_slot`: each device l reads all 4 slots of each of 64 source devices, each slot for exactly one of its LES lines.
All inputs are finite; a program needn't handle non-finite values.
Results may differ from the reference program's by a relative error of at most 0.001.
Values may be sent and summed in bfloat16 or wider, within the bound.
No kernel may reach another device: no remote copies, remote signals or barrier semaphores. Data moves between devices by JAX's collectives and lax.ppermute only.
A program may use at most 64 MiB of HBM per device.

```python
import math
import jax
import jax.numpy as jnp
from jax import lax

GX = 16
GY = 32
ZC = 128
REGIONS = 16
NX = 256
NY = 256
LX = 8
LY = 32
NXL = 128
NYL = 256
NB = 512
NL = 256
PEERS = 128
CAP = 4
N_WIDE = 16
N_NARROW = 8


def pick_sources(key):
    first, second = jax.random.split(key)
    heaviness = jax.random.randint(first, (PEERS,), 0, 3)
    weight = jnp.where(heaviness == 0, 1, jnp.where(heaviness == 1, 2, 4)).astype(jnp.int32)
    raw = jax.random.randint(second, (PEERS, PEERS), 0, 65536).astype(jnp.int32) * weight[None, :]
    raw = raw.at[0, 0].set(262144).at[0, PEERS - 1].set(262144)
    score = raw * PEERS + jnp.arange(PEERS, dtype=jnp.int32)[None, :]
    chosen = jnp.sort(lax.top_k(score, PEERS // 2)[1], axis=1).astype(jnp.int32)
    rows_idx = jnp.arange(PEERS, dtype=jnp.int32)[:, None]
    taken = jnp.zeros((PEERS, PEERS), jnp.int32).at[rows_idx, chosen].set(1)
    return (taken, chosen)


def draw_send_lines(key, part):
    taken, chosen = pick_sources(key)
    key = jax.random.fold_in(key, 5)
    rank = jnp.cumsum(taken, axis=0) - taken
    keys = jax.random.split(key, PEERS)
    inner = jax.vmap(lambda one: jax.random.permutation(one, jnp.arange(1, NB - 1, dtype=jnp.int32)))(keys)
    order = jnp.concatenate([jnp.full((PEERS, 1), NB - 1, jnp.int32), jnp.zeros((PEERS, 1), jnp.int32), inner], axis=1)
    position = rank.T[:, :, None] * CAP + jnp.arange(CAP, dtype=jnp.int32)[None, None, :]
    sender = jnp.arange(PEERS, dtype=jnp.int32)[:, None, None]
    return order[sender, position].astype(jnp.int32)


def draw_recv_slot(key, part):
    taken, chosen = pick_sources(key)
    key = jax.random.fold_in(key, 9)
    slots = (chosen[:, :, None] * CAP + jnp.arange(CAP, dtype=jnp.int32)[None, None, :]).reshape(PEERS, NL)
    keys = jax.random.split(key, PEERS)
    perms = jax.vmap(lambda one: jax.random.permutation(one, NL))(keys)
    return jnp.take_along_axis(slots, perms.astype(jnp.int32), axis=1).astype(jnp.int32)


def place_ends(entries, stream_key, least, largest):
    dims = entries.shape
    place = [jax.random.randint(jax.random.fold_in(stream_key, axis), (), 0, dims[axis]) for axis in range(len(dims))]
    entries = entries.at[tuple(place)].set(least)
    longest = dims.index(max(dims))
    place[longest] = (place[longest] + 1) % dims[longest]
    return entries.at[tuple(place)].set(largest)


def shard_levels(rng, extent, cuts, smallest, high):
    gain = 1.0
    for dim, blocks in cuts:
        steps = jax.random.uniform(jax.random.fold_in(jax.random.fold_in(rng, 6), dim), (blocks,), jnp.float32, smallest / len(cuts), high / len(cuts))
        gain = gain * jnp.repeat(jnp.exp(steps), extent[dim] // blocks).reshape((-1,) + (1,) * (len(extent) - 1 - dim))
    return gain


def gaussian(rng, dims, scale, reach, cuts=(), held_as=jnp.bfloat16):
    entries = jax.random.normal(rng, dims, jnp.float32) * scale
    if len(cuts) > 0:
        entries = shard_levels(rng, dims, cuts, -0.22, 0.18) * entries
    return jnp.clip(entries, min=-reach, max=reach).astype(held_as)


def setup_inputs(seed: int = 0) -> dict:
    splits = jax.random.split(jax.random.key(seed), 8)
    potential = gaussian(splits[0], (8, NX, NY, ZC), 1.0, 6.0, ((1, 16), (2, 8)), jnp.float32)
    source_current = gaussian(splits[1], (3, NX, NY, ZC), 1.0, 6.0, ((1, 16), (2, 8)), jnp.float32)
    cell_label = place_ends(jax.random.randint(splits[2], (NX, NY, ZC), 0, 3 * REGIONS), jax.random.fold_in(splits[2], 1), 0, (3 * REGIONS) - 1).astype(jnp.int32)
    region_kappa = jnp.clip(jnp.exp(jax.random.uniform(splits[3], (REGIONS,), jnp.float32, math.log(0.5), math.log(4.0))), 0.5, 4.0)
    send_lines = draw_send_lines(jax.random.fold_in(splits[7], 71), 0)
    recv_slot = draw_recv_slot(jax.random.fold_in(splits[7], 71), 0)
    velocity = gaussian(splits[6], (3, NXL, NYL, ZC), 1.0, 6.0, ((1, 16), (2, 8)), jnp.float32)
    return {"potential": potential, "source_current": source_current, "cell_label": cell_label, "region_kappa": region_kappa, "send_lines": send_lines, "recv_slot": recv_slot, "velocity": velocity}


DT = 0.25
VISC = 0.5


def beside_all(q):
    ends = jnp.pad(q[1:-1, 1:-1], ((0, 0), (0, 0), (1, 1)))
    return q[2:, 1:-1] + q[:-2, 1:-1] + q[1:-1, 2:] + q[1:-1, :-2] + ends[:, :, 2:] + ends[:, :, :-2]


def slope(q, axis):
    if axis == 0:
        return 0.5 * (q[2:, 1:-1] - q[:-2, 1:-1])
    if axis == 1:
        return 0.5 * (q[1:-1, 2:] - q[1:-1, :-2])
    ends = jnp.pad(q[1:-1, 1:-1], ((0, 0), (0, 0), (1, 1)))
    return 0.5 * (ends[:, :, 2:] - ends[:, :, :-2])


def sweep(padded, kappa, drive):
    scale = 1.0 / (36.0 + kappa * kappa)
    div_re = slope(padded[0], 0) + slope(padded[1], 1) + slope(padded[2], 2)
    div_im = slope(padded[4], 0) + slope(padded[5], 1) + slope(padded[6], 2)
    real_parts = []
    imag_parts = []
    for comp in range(3):
        first = drive[comp] + beside_all(padded[comp]) + kappa * slope(padded[7], comp)
        second = beside_all(padded[4 + comp]) - kappa * slope(padded[3], comp)
        real_parts.append((6.0 * first + kappa * second) * scale)
        imag_parts.append((6.0 * second - kappa * first) * scale)
    first = beside_all(padded[3]) + kappa * div_im
    second = beside_all(padded[7]) - kappa * div_re
    real_parts.append((6.0 * first + kappa * second) * scale)
    imag_parts.append((6.0 * second - kappa * first) * scale)
    return jnp.stack(real_parts + imag_parts)


def curl(padded, base):
    ax_f, ay_f, az_f = padded[base], padded[base + 1], padded[base + 2]
    return [slope(az_f, 1) - slope(ay_f, 2), slope(ax_f, 2) - slope(az_f, 0), slope(ay_f, 0) - slope(ax_f, 1)]


def lorentz_force(padded, kappa, drive, melt):
    real_b = curl(padded, 0)
    imag_b = curl(padded, 4)
    cur_re = []
    cur_im = []
    for comp in range(3):
        field_re = padded[comp, 1:-1, 1:-1] + slope(padded[3], comp)
        field_im = padded[4 + comp, 1:-1, 1:-1] + slope(padded[7], comp)
        cur_re.append(drive[comp] + kappa * field_im)
        cur_im.append(-kappa * field_re)
    parts = []
    for comp in range(3):
        nxt = (comp + 1) % 3
        far = (comp + 2) % 3
        value = cur_re[nxt] * real_b[far] + cur_im[nxt] * imag_b[far] - cur_re[far] * real_b[nxt] - cur_im[far] * imag_b[nxt]
        parts.append(0.5 * value * melt)
    return jnp.stack(parts).astype(jnp.bfloat16)


def predict(padded, push):
    rows_out = []
    for comp in range(3):
        middle = padded[comp, 1:-1, 1:-1]
        carried = padded[0, 1:-1, 1:-1] * slope(padded[comp], 0)
        carried = carried + padded[1, 1:-1, 1:-1] * slope(padded[comp], 1)
        carried = carried + padded[2, 1:-1, 1:-1] * slope(padded[comp], 2)
        spread = beside_all(padded[comp]) - 6.0 * middle
        rows_out.append(middle + DT * (-carried + VISC * spread + push[comp].astype(jnp.float32)))
    return jnp.stack(rows_out)


def pad_plane(field):
    return jnp.pad(field, ((0, 0), (1, 1), (1, 1), (0, 0)))


def reference(potential, source_current, cell_label, region_kappa, send_lines, recv_slot, velocity):
    material = (cell_label // REGIONS).astype(jnp.int32)
    region = (cell_label % REGIONS).astype(jnp.int32)
    kappa = jnp.where(material == 2, jnp.take(region_kappa, region), 0.0).astype(potential.dtype)
    drive = jnp.where((material == 0)[None], source_current, 0.0)
    melt = (material == 2).astype(potential.dtype)
    potential_half = sweep(pad_plane(potential), kappa, drive)
    potential_next = sweep(pad_plane(potential_half), kappa, drive)
    lorentz = lorentz_force(pad_plane(potential_next), kappa, drive, melt)
    source_dev = (recv_slot // CAP).astype(jnp.int32)
    slot_in = (recv_slot % CAP).astype(jnp.int32)
    target = jnp.arange(PEERS, dtype=jnp.int32)[:, None]
    line = send_lines[source_dev, target, slot_in]
    grid_x = (source_dev // N_NARROW) * GX + line // GY
    grid_y = (source_dev % N_NARROW) * GY + line % GY
    picked = lorentz[:, grid_x, grid_y, :]
    picked = picked.reshape(3, N_WIDE, N_NARROW, LX, LY, ZC).transpose(0, 1, 3, 2, 4, 5)
    les_force = picked.reshape(3, NXL, NYL, ZC)
    velocity_next = predict(pad_plane(velocity), les_force)
    return potential_next, les_force, velocity_next
```

```python
import functools

import jax
import jax.numpy as jnp
from jax import lax
from jax.experimental import pallas as pl
from jax.experimental.pallas import tpu as pltpu
from jax.sharding import PartitionSpec as P

DT = 0.25
VISC = 0.5
F32 = jnp.float32
BF16 = jnp.bfloat16
DEEP = 3
FLAT = 2
ROWS = 48
OFF = 8
MIB = 1 << 20


def strip(start, size, stride):
    return pl.ds(start, size, stride=stride)


def planes_of(span_x, span_y):
    return 8 * DEEP + 4 * FLAT


def prep_kernel(span_x, span_y, regions, rk, pot, src, lab, vel, dk, wlo, whi, nlo, nhi, vwlo, vwhi, vnlo, vnhi):
    depth = pot.shape[-1]

    def plane(x, carry):
        rows = pl.ds(pl.multiple_of(x * span_y, span_y), span_y)
        label = lab[rows, :]
        kappa = jnp.zeros((span_y, depth), F32)
        for r in range(regions):
            kappa = jnp.where(label == 2 * regions + r, rk[r], kappa)
        coil = label < regions
        for c in range(3):
            dk[c, rows, :] = jnp.where(coil, src[c, rows, :], 0.0)
        dk[3, rows, :] = kappa
        return carry

    lax.fori_loop(0, span_x, plane, 0)
    for c in range(8):
        for d in range(DEEP):
            wlo[c * DEEP + d] = pot[c, pl.ds(d * span_y, span_y), :]
            whi[c * DEEP + d] = pot[c, pl.ds((span_x - 1 - d) * span_y, span_y), :]
            nlo[c * DEEP + d] = pot[c, strip(d, span_x, span_y), :]
            nhi[c * DEEP + d] = pot[c, strip(span_y - 1 - d, span_x, span_y), :]
    for f in range(4):
        for d in range(FLAT):
            p = 8 * DEEP + f * FLAT + d
            wlo[p] = dk[f, pl.ds(d * span_y, span_y), :]
            whi[p] = dk[f, pl.ds((span_x - 1 - d) * span_y, span_y), :]
            nlo[p] = dk[f, strip(d, span_x, span_y), :]
            nhi[p] = dk[f, strip(span_y - 1 - d, span_x, span_y), :]
    les_x = vel.shape[1] // span_y
    for c in range(3):
        vwlo[c] = vel[c, pl.ds(0, span_y), :]
        vwhi[c] = vel[c, pl.ds((les_x - 1) * span_y, span_y), :]
        vnlo[c] = vel[c, strip(0, les_x, span_y), :]
        vnhi[c] = vel[c, strip(span_y - 1, les_x, span_y), :]


def corner_kernel(span_x, nlo, nhi, clo, chi):
    planes = nlo.shape[0]
    for d in range(FLAT):
        for side, ref in enumerate((nlo, nhi)):
            rows = pl.ds((d * 2 + side) * planes, planes)
            clo[rows, :] = ref[:, d, :]
            chi[rows, :] = ref[:, span_x - 1 - d, :]


def lanes(value):
    depth = value.shape[-1]
    lane = lax.broadcasted_iota(jnp.int32, value.shape, 1)
    ahead = jnp.where(lane == depth - 1, 0.0, pltpu.roll(value, depth - 1, 1))
    back = jnp.where(lane == 0, 0.0, pltpu.roll(value, 1, 1))
    return ahead, back


def sweep_tile(old, new, field, row):
    s6 = 6.0 * field[4, pl.ds(row, 8), :]
    kappa = field[3, pl.ds(row, 8), :]
    sk = kappa * field[4, pl.ds(row, 8), :]
    half = 0.5 * kappa
    total = []
    diff = []
    for c in range(8):
        xf = old[c, pl.ds(row + ROWS, 8), :]
        xb = old[c, pl.ds(row - ROWS, 8), :]
        yf = old[c, pl.ds(row + 1, 8), :]
        yb = old[c, pl.ds(row - 1, 8), :]
        zf, zb = lanes(old[c, pl.ds(row, 8), :])
        total.append((xf + xb) + (yf + yb) + (zf + zb))
        if c % 4 == 3:
            diff.append((xf - xb, yf - yb, zf - zb))
        else:
            diff.append(((xf - xb), (yf - yb), (zf - zb))[c % 4])
    for c in range(3):
        first = (field[c, pl.ds(row, 8), :] + total[c]) + half * diff[7][c]
        second = total[4 + c] - half * diff[3][c]
        new[c, pl.ds(row, 8), :] = s6 * first + sk * second
        new[4 + c, pl.ds(row, 8), :] = s6 * second - sk * first
    first = total[3] + half * (diff[4] + diff[5] + diff[6])
    second = total[7] - half * (diff[0] + diff[1] + diff[2])
    new[3, pl.ds(row, 8), :] = s6 * first + sk * second
    new[7, pl.ds(row, 8), :] = s6 * second - sk * first


def lorentz_tile(now, field, row):
    def grab(c, shift):
        return now[c, pl.ds(row + shift, 8), :]

    kappa = field[3, pl.ds(row, 8), :]

    def part(base):
        a = [grab(base + c, 0) for c in range(3)]
        azf, azb = lanes(a[0])
        bzf, bzb = lanes(a[1])
        curl = [
            (grab(base + 2, 1) - grab(base + 2, -1)) - (bzf - bzb),
            (azf - azb) - (grab(base + 2, ROWS) - grab(base + 2, -ROWS)),
            (grab(base + 1, ROWS) - grab(base + 1, -ROWS)) - (grab(base, 1) - grab(base, -1)),
        ]
        phi = grab(base + 3, 0)
        pzf, pzb = lanes(phi)
        grad = [
            grab(base + 3, ROWS) - grab(base + 3, -ROWS),
            grab(base + 3, 1) - grab(base + 3, -1),
            pzf - pzb,
        ]
        return curl, [a[c] + 0.5 * grad[c] for c in range(3)], a + [phi]

    real_b, field_re, values_re = part(0)
    imag_b, field_im, values_im = part(4)
    cur_re = [field[c, pl.ds(row, 8), :] + kappa * field_im[c] for c in range(3)]
    cur_im = [-kappa * field_re[c] for c in range(3)]
    force = []
    for c in range(3):
        n = (c + 1) % 3
        f = (c + 2) % 3
        value = (cur_re[n] * real_b[f] - cur_re[f] * real_b[n]) + (
            cur_im[n] * imag_b[f] - cur_im[f] * imag_b[n]
        )
        force.append(jnp.where(kappa > 0.0, 0.25 * value, 0.0))
    return force, values_re + values_im


def main_kernel(
    span_x, span_y, slots, flags, pot, dk, wlo, whi, nlo, nhi, clo, chi, hot, nxt, out, s0, s1, s2, field, force
):
    depth = pot.shape[-1]
    planes = wlo.shape[0]

    def at(x):
        return (x + DEEP) * ROWS + OFF

    def lay(x, carry):
        rows = pl.ds(pl.multiple_of(x * span_y, span_y), span_y)
        there = pl.ds(pl.multiple_of((x + DEEP) * ROWS + OFF, 8), span_y)
        for c in range(8):
            s0[c, there, :] = pot[c, rows, :]
        for f in range(4):
            field[f, there, :] = dk[f, rows, :]
        return carry

    lax.fori_loop(0, span_x, lay, 0)
    for c in range(12):
        deep = DEEP if c < 8 else FLAT
        ref, part = (s0, c) if c < 8 else (field, c - 8)
        for d in range(deep):
            p = c * DEEP + d if c < 8 else 8 * DEEP + part * FLAT + d
            ref[part, pl.ds(at(-1 - d), span_y), :] = wlo[p]
            ref[part, pl.ds(at(span_x + d), span_y), :] = whi[p]
            ref[part, strip(at(0) - 1 - d, span_x, ROWS), :] = nlo[p]
            ref[part, strip(at(0) + span_y + d, span_x, ROWS), :] = nhi[p]
            for e in range(deep - 1 - d):
                for source, x in ((clo, -1 - e), (chi, span_x + e)):
                    ref[part, pl.ds(at(x) - 1 - d, 1), :] = source[pl.ds(e * 2 * planes + p, 1), :]
                    ref[part, pl.ds(at(x) + span_y + d, 1), :] = source[pl.ds((e * 2 + 1) * planes + p, 1), :]

    line = lax.broadcasted_iota(jnp.int32, (8, depth), 0)

    def scale(i, carry):
        x = i - FLAT
        fx = jnp.where(x < 0, flags[0], jnp.where(x >= span_x, flags[1], 1.0))
        for t in range(5):
            row = at(x) - FLAT + 8 * t
            y = line + (8 * t - FLAT)
            fy = jnp.where(y < 0, flags[2], jnp.where(y >= span_y, flags[3], 1.0))
            kappa = field[3, pl.ds(row, 8), :]
            field[4, pl.ds(row, 8), :] = (fx * fy) / (36.0 + kappa * kappa)
        return carry

    lax.fori_loop(0, span_x + 2 * FLAT, scale, 0)

    def first(i, carry):
        for t in range(5):
            sweep_tile(s0, s1, field, at(i - 2) - 2 + 8 * t)
        return carry

    lax.fori_loop(0, span_x + 4, first, 0)

    def second(i, carry):
        for t in range(5):
            sweep_tile(s1, s2, field, at(i - 1) - 1 + 8 * t)
        return carry

    lax.fori_loop(0, span_x + 2, second, 0)

    def third(x, carry):
        for t in range(span_y // 8):
            f, values = lorentz_tile(s2, field, at(x) + 8 * t)
            rows = pl.ds(pl.multiple_of(x * span_y + 8 * t, 8), 8)
            for c in range(3):
                force[c, rows, :] = f[c]
            for c in range(8):
                nxt[c, rows, :] = values[c]
        return carry

    lax.fori_loop(0, span_x, third, 0)

    table = [force[c].astype(BF16) for c in range(3)]
    chunk = 256
    upper = lax.broadcasted_iota(jnp.int32, (chunk // 8, 8, depth), 1) < slots

    def pick(i, carry):
        h = hot[pl.ds(pl.multiple_of(i * chunk, chunk), chunk), :]
        got = [
            jnp.dot(h, table[c], preferred_element_type=F32).reshape(chunk // 8, 8, depth)
            for c in range(3)
        ]
        both = jnp.concatenate([jnp.where(upper, got[0], got[1]), got[2]], axis=1)
        out[pl.ds(i * (chunk // 8), chunk // 8)] = both.astype(BF16)
        return carry

    lax.fori_loop(0, hot.shape[0] // chunk, pick, 0)


def flow_kernel(les_x, span_y, vel, vwlo, vwhi, vnlo, vnhi, base, s0):
    def at(x):
        return (x + 1) * ROWS + OFF

    for c in range(3):
        for x in range(les_x):
            s0[c, pl.ds(at(x), span_y), :] = vel[c, pl.ds(x * span_y, span_y), :]
        s0[c, pl.ds(at(-1), span_y), :] = vwlo[c]
        s0[c, pl.ds(at(les_x), span_y), :] = vwhi[c]
        s0[c, strip(at(0) - 1, les_x, ROWS), :] = vnlo[c]
        s0[c, strip(at(0) + span_y, les_x, ROWS), :] = vnhi[c]

    def step(x, carry):
        for t in range(span_y // 8):
            row = at(x) + 8 * t
            middle = [s0[c, pl.ds(row, 8), :] for c in range(3)]
            for c in range(3):
                xf = s0[c, pl.ds(row + ROWS, 8), :]
                xb = s0[c, pl.ds(row - ROWS, 8), :]
                yf = s0[c, pl.ds(row + 1, 8), :]
                yb = s0[c, pl.ds(row - 1, 8), :]
                zf, zb = lanes(middle[c])
                carried = 0.5 * (middle[0] * (xf - xb) + middle[1] * (yf - yb) + middle[2] * (zf - zb))
                spread = (xf + xb) + (yf + yb) + (zf + zb) - 6.0 * middle[c]
                base[c, pl.ds(pl.multiple_of(x * span_y + 8 * t, 8), 8), :] = middle[c] + DT * (
                    VISC * spread - carried
                )
        return carry

    lax.fori_loop(0, les_x, step, 0)


def last_kernel(hot, got, base, les, nxt):
    rows = got.shape[0] * got.shape[1]
    values = got[...].reshape(rows, got.shape[2])
    push = jnp.dot(hot[...], values, preferred_element_type=F32).astype(BF16)
    les[...] = push
    nxt[...] = base[...] + DT * push.astype(F32)


def call(kernel, out, name, scratch=(), smem=0, count=1, limit=48):
    vmem = pl.BlockSpec(memory_space=pltpu.VMEM)
    specs = [pl.BlockSpec(memory_space=pltpu.SMEM)] * smem + [vmem] * (count - smem)
    return pl.pallas_call(
        kernel,
        out_shape=[jax.ShapeDtypeStruct(shape, kind) for shape, kind in out],
        in_specs=specs,
        out_specs=[vmem] * len(out),
        scratch_shapes=[pltpu.VMEM(shape, kind) for shape, kind in scratch],
        compiler_params=pltpu.CompilerParams(vmem_limit_bytes=limit * MIB),
        name=name,
    )


def swap(low, high, axis):
    count = lax.axis_size(axis)
    forward = [(i, i + 1) for i in range(count - 1)]
    backward = [(target, source) for source, target in forward]
    return lax.ppermute(high, axis, forward), lax.ppermute(low, axis, backward)


def body(potential, source_current, cell_label, region_kappa, send_lines, recv_slot, velocity):
    _, span_x, span_y, depth = potential.shape
    les_x = velocity.shape[1]
    peers, slots = send_lines.shape[1:]
    cells = span_x * span_y
    lines = les_x * span_y
    planes = planes_of(span_x, span_y)
    pot = potential.reshape(8, cells, depth)
    src = source_current.reshape(3, cells, depth)
    lab = cell_label.reshape(cells, depth)
    vel = velocity.reshape(3, lines, depth)

    wide = ((planes, span_y, depth), F32)
    narrow = ((planes, span_x, depth), F32)
    vw = ((3, span_y, depth), F32)
    vn = ((3, les_x, depth), F32)
    dk, wlo, whi, nlo, nhi, vwlo, vwhi, vnlo, vnhi = call(
        functools.partial(prep_kernel, span_x, span_y, region_kappa.shape[0]),
        [((4, cells, depth), F32), wide, wide, narrow, narrow, vw, vw, vn, vn],
        "prep", smem=1, count=5,
    )(region_kappa, pot, src, lab, vel)

    wlo, whi = swap(wlo, whi, "wide")
    nlo, nhi = swap(nlo, nhi, "narrow")
    corner = ((FLAT * 2 * planes, depth), F32)
    clo, chi = call(
        functools.partial(corner_kernel, span_x), [corner, corner], "corner", count=2
    )(nlo, nhi)
    clo, chi = swap(clo, chi, "wide")
    vwlo, vwhi = swap(vwlo, vwhi, "wide")
    vnlo, vnhi = swap(vnlo, vnhi, "narrow")

    sent = jnp.concatenate([send_lines[0], send_lines[0]], axis=1).reshape(-1)
    hot = (sent[:, None] == jnp.arange(cells, dtype=jnp.int32)[None, :]).astype(BF16)
    slot = recv_slot[0]
    place = (slot // slots) * 16 + slot % slots
    want = (place[None, :] + slots * jnp.arange(3, dtype=jnp.int32)[:, None]).reshape(-1)
    take = (want[:, None] == jnp.arange(peers * 16, dtype=jnp.int32)[None, :]).astype(BF16)

    w, n = lax.axis_index("wide"), lax.axis_index("narrow")
    flags = jnp.stack(
        [w > 0, w < lax.axis_size("wide") - 1, n > 0, n < lax.axis_size("narrow") - 1]
    ).astype(F32)
    pad = (span_x + 2 * DEEP) * ROWS
    potential_next, outgoing = call(
        functools.partial(main_kernel, span_x, span_y, slots),
        [((8, cells, depth), F32), ((peers, 16, depth), BF16)],
        "sweeps",
        scratch=[((8, pad, depth), F32)] * 3 + [((5, pad, depth), F32), ((3, cells, depth), F32)],
        smem=1, count=10,
    )(flags, pot, dk, wlo, whi, nlo, nhi, clo, chi, hot)

    incoming = lax.all_to_all(
        outgoing, ("wide", "narrow"), split_axis=0, concat_axis=0, tiled=True
    )
    (base,) = call(
        functools.partial(flow_kernel, les_x, span_y),
        [((3, lines, depth), F32)],
        "flow",
        scratch=[((3, (les_x + 2) * ROWS, depth), F32)],
        count=5,
    )(vel, vwlo, vwhi, vnlo, vnhi)
    les, velocity_next = call(
        last_kernel,
        [((3 * lines, depth), BF16), ((3 * lines, depth), F32)],
        "last", count=3,
    )(take, incoming, base.reshape(3 * lines, depth))
    block = (3, les_x, span_y, depth)
    return potential_next.reshape(potential.shape), les.reshape(block), velocity_next.reshape(block)


def solution(mesh):
    in_specs = (
        P(None, "wide", "narrow", None),
        P(None, "wide", "narrow", None),
        P("wide", "narrow", None),
        P(),
        P(("wide", "narrow"), None, None),
        P(("wide", "narrow"), None),
        P(None, "wide", "narrow", None),
    )
    out_specs = (
        P(None, "wide", "narrow", None),
        P(None, "wide", "narrow", None),
        P(None, "wide", "narrow", None),
    )
    return jax.shard_map(body, mesh=mesh, in_specs=in_specs, out_specs=out_specs, check_vma=False)
```

```python
import functools

import jax
import jax.numpy as jnp
from jax import lax
from jax.experimental import pallas as pl
from jax.experimental.pallas import tpu as pltpu
from jax.sharding import PartitionSpec as P

DT = 0.25
VISC = 0.5
F32 = jnp.float32
BF16 = jnp.bfloat16
DEEP = 3
FLAT = 2
ROWS = 40
OFF = 8
MIB = 1 << 20
LIMIT_IN = 48
LIMIT_OUT = 48


def strip(start, size, stride):
    return pl.ds(start, size, stride=stride)


def planes_of():
    return 8 * DEEP + 4 * FLAT + 3


def kappa_of(label, rk, regions):
    kappa = jnp.zeros(label.shape, F32)
    for r in range(regions):
        kappa = jnp.where(label == 2 * regions + r, rk[r], kappa)
    return kappa


class Copies:
    def __init__(self, sems):
        self.sems = sems
        self.count = 0

    def start(self, source, target):
        one = pltpu.make_async_copy(source, target, self.sems.at[self.count])
        one.start()
        self.count += 1
        return one


def faces_kernel(
    span_x, span_y, regions, rk, pot, src, lab, vel, wlo, whi, nlo, nhi, all_pot, all_src, all_lab, all_vel, sems
):
    les_x = vel.shape[1]
    flow = 8 * DEEP + 4 * FLAT
    copies = Copies(sems)
    waits = [
        copies.start(source, target)
        for source, target in ((lab, all_lab), (src, all_src), (vel, all_vel), (pot, all_pot))
    ]
    for one in waits[:2]:
        one.wait()
    for side, (wide, narrow) in enumerate(((wlo, nlo), (whi, nhi))):
        for d in range(FLAT):
            x = span_x - FLAT + d if side else d
            y = span_y - 1 - d if side else d
            label = all_lab[x]
            for c in range(3):
                wide[8 * DEEP + 4 * d + c] = jnp.where(label < regions, all_src[c, x], 0.0)
            wide[8 * DEEP + 4 * d + 3] = kappa_of(label, rk, regions)
            label = all_lab[:, y, :]
            for c in range(3):
                narrow[8 * DEEP + 4 * d + c] = jnp.where(label < regions, all_src[c, :, y, :], 0.0)
            narrow[8 * DEEP + 4 * d + 3] = kappa_of(label, rk, regions)
    waits[2].wait()
    for side, (wide, narrow) in enumerate(((wlo, nlo), (whi, nhi))):
        for c in range(3):
            wide[flow + c] = all_vel[c, side * (les_x - 1)]
            narrow[flow + c, pl.ds(0, les_x), :] = all_vel[c, :, side * (span_y - 1), :]
            narrow[flow + c, pl.ds(les_x, span_x - les_x), :] = jnp.zeros((span_x - les_x, vel.shape[3]), F32)
    waits[3].wait()
    for side, (wide, narrow) in enumerate(((wlo, nlo), (whi, nhi))):
        for d in range(DEEP):
            x = span_x - DEEP + d if side else d
            y = span_y - 1 - d if side else d
            for c in range(8):
                wide[8 * d + c] = all_pot[c, x]
                narrow[8 * d + c] = all_pot[c, :, y, :]


def corner_kernel(span_x, nlo, nhi, clo, chi):
    planes = 8 * DEEP + 4 * FLAT
    for d in range(FLAT):
        for side, ref in enumerate((nlo, nhi)):
            rows = pl.ds((d * 2 + side) * planes, planes)
            clo[rows, :] = ref[:planes, d, :]
            chi[rows, :] = ref[:planes, span_x - 1 - d, :]


def place(c, d):
    return 8 * d + c if c < 8 else 8 * DEEP + 4 * d + c - 8


def at(x):
    return (x + DEEP) * ROWS + OFF


def scale_plane(span_x, span_y, flags, field, x):
    line = lax.broadcasted_iota(jnp.int32, (8, field.shape[-1]), 0)
    fx = jnp.where(x < 0, flags[0], jnp.where(x >= span_x, flags[1], 1.0))
    for t in range(5):
        row = at(x) - FLAT + 8 * t
        y = line + (8 * t - FLAT)
        fy = jnp.where(y < 0, flags[2], jnp.where(y >= span_y, flags[3], 1.0))
        kappa = field[3, pl.ds(row, 8), :]
        field[4, pl.ds(row, 8), :] = (fx * fy) / (36.0 + kappa * kappa)


def sweep_plane(old, new, field, x, margin):
    for t in range(5):
        sweep_tile(old, new, field, at(x) - margin + 8 * t)


def over(low, high, do):
    def step(i, carry):
        do(i + low)
        return carry

    lax.fori_loop(0, high - low, step, 0)


def lanes(value):
    depth = value.shape[-1]
    lane = lax.broadcasted_iota(jnp.int32, value.shape, 1)
    ahead = jnp.where(lane == depth - 1, 0.0, pltpu.roll(value, depth - 1, 1))
    back = jnp.where(lane == 0, 0.0, pltpu.roll(value, 1, 1))
    return ahead, back


def sweep_tile(old, new, field, row):
    s6 = 6.0 * field[4, pl.ds(row, 8), :]
    kappa = field[3, pl.ds(row, 8), :]
    sk = kappa * field[4, pl.ds(row, 8), :]
    half = 0.5 * kappa
    total = []
    diff = []
    for c in range(8):
        xf = old[c, pl.ds(row + ROWS, 8), :]
        xb = old[c, pl.ds(row - ROWS, 8), :]
        yf = old[c, pl.ds(row + 1, 8), :]
        yb = old[c, pl.ds(row - 1, 8), :]
        zf, zb = lanes(old[c, pl.ds(row, 8), :])
        total.append((xf + xb) + (yf + yb) + (zf + zb))
        if c % 4 == 3:
            diff.append((xf - xb, yf - yb, zf - zb))
        else:
            diff.append(((xf - xb), (yf - yb), (zf - zb))[c % 4])
    for c in range(3):
        first = (field[c, pl.ds(row, 8), :] + total[c]) + half * diff[7][c]
        second = total[4 + c] - half * diff[3][c]
        new[c, pl.ds(row, 8), :] = s6 * first + sk * second
        new[4 + c, pl.ds(row, 8), :] = s6 * second - sk * first
    first = total[3] + half * (diff[4] + diff[5] + diff[6])
    second = total[7] - half * (diff[0] + diff[1] + diff[2])
    new[3, pl.ds(row, 8), :] = s6 * first + sk * second
    new[7, pl.ds(row, 8), :] = s6 * second - sk * first


def lorentz_tile(now, field, row):
    def grab(c, shift):
        return now[c, pl.ds(row + shift, 8), :]

    kappa = field[3, pl.ds(row, 8), :]

    def part(base):
        a = [grab(base + c, 0) for c in range(3)]
        azf, azb = lanes(a[0])
        bzf, bzb = lanes(a[1])
        curl = [
            (grab(base + 2, 1) - grab(base + 2, -1)) - (bzf - bzb),
            (azf - azb) - (grab(base + 2, ROWS) - grab(base + 2, -ROWS)),
            (grab(base + 1, ROWS) - grab(base + 1, -ROWS)) - (grab(base, 1) - grab(base, -1)),
        ]
        phi = grab(base + 3, 0)
        pzf, pzb = lanes(phi)
        grad = [
            grab(base + 3, ROWS) - grab(base + 3, -ROWS),
            grab(base + 3, 1) - grab(base + 3, -1),
            pzf - pzb,
        ]
        return curl, [a[c] + 0.5 * grad[c] for c in range(3)]

    real_b, field_re = part(0)
    imag_b, field_im = part(4)
    cur_re = [field[c, pl.ds(row, 8), :] + kappa * field_im[c] for c in range(3)]
    cur_im = [-kappa * field_re[c] for c in range(3)]
    force = []
    for c in range(3):
        n = (c + 1) % 3
        f = (c + 2) % 3
        value = (cur_re[n] * real_b[f] - cur_re[f] * real_b[n]) + (
            cur_im[n] * imag_b[f] - cur_im[f] * imag_b[n]
        )
        force.append(jnp.where(kappa > 0.0, 0.25 * value, 0.0))
    return force


def force_plane(now, field, force, span_y, x):
    for t in range(span_y // 8):
        f = lorentz_tile(now, field, at(x) + 8 * t)
        rows = pl.ds(pl.multiple_of(x * span_y + 8 * t, 8), 8)
        for c in range(3):
            force[c, rows, :] = f[c]


def stored(x):
    return pl.ds((x + DEEP) * ROWS, ROWS + OFF)


def kept(i):
    return pl.ds(i * (ROWS + OFF), ROWS + OFF)


def inner_kernel(
    span_x, span_y, regions, flags, rk, pot, src, lab, nlo, nhi,
    nxt, halves, nexts, fields, force, s0, s1, s2, field, some, tags, sems,
):
    copies = Copies(sems)
    early = [copies.start(lab, tags), copies.start(src, some)]
    late = [
        copies.start(pot.at[:, x], s0.at[:, pl.ds(at(x), span_y), :]) for x in range(span_x)
    ]
    for c in range(12):
        deep = DEEP if c < 8 else FLAT
        ref, part = (s0, c) if c < 8 else (field, c - 8)
        for d in range(deep):
            ref[part, strip(at(0) - 1 - d, span_x, ROWS), :] = nlo[place(c, d)]
            ref[part, strip(at(0) + span_y + d, span_x, ROWS), :] = nhi[place(c, d)]
    for one in early:
        one.wait()

    def lay(x):
        there = pl.ds(pl.multiple_of((x + DEEP) * ROWS + OFF, 8), span_y)
        label = tags[x]
        for c in range(3):
            field[c, there, :] = jnp.where(label < regions, some[c, x], 0.0)
        field[3, there, :] = kappa_of(label, rk, regions)

    over(0, span_x, lay)
    over(0, span_x, lambda x: scale_plane(span_x, span_y, flags, field, x))
    for one in late:
        one.wait()
    over(1, span_x - 1, lambda x: sweep_plane(s0, s1, field, x, 2))
    over(2, span_x - 2, lambda x: sweep_plane(s1, s2, field, x, 1))
    done = [
        copies.start(s2.at[:, pl.ds(at(x), span_y), :], nxt.at[:, x]) for x in range(2, span_x - 2)
    ]
    over(3, span_x - 3, lambda x: force_plane(s2, field, force, span_y, x))
    for c in range(8):
        for i, x in enumerate((1, 2, span_x - 3, span_x - 2)):
            halves[c, kept(i), :] = s1[c, stored(x), :]
        for i, x in enumerate((2, 3, span_x - 4, span_x - 3)):
            nexts[c, kept(i), :] = s2[c, stored(x), :]
    for c in range(5):
        for i, x in enumerate((0, 1, 2, span_x - 3, span_x - 2, span_x - 1)):
            fields[c, kept(i), :] = field[c, stored(x), :]
    for one in done:
        one.wait()


def outer_kernel(
    span_x, span_y, slots, flags, pot, wlo, whi, nlo, nhi, clo, chi, hot, halves, nexts, fields, some_force, old_nxt,
    nxt, out, s0, s1, s2, field, force, sent, sems, sent_sems,
):
    depth = pot.shape[-1]
    planes = 8 * DEEP + 4 * FLAT
    copies = Copies(sems)
    early = []
    late = []
    for d in range(FLAT):
        for ref, x in ((wlo, d - FLAT), (whi, span_x + d)):
            early.append(
                copies.start(ref.at[pl.ds(8 * DEEP + 4 * d, 4)], field.at[pl.ds(0, 4), pl.ds(at(x), span_y), :])
            )
    for d in range(DEEP):
        for ref, x in ((wlo, d - DEEP), (whi, span_x + d)):
            late.append(copies.start(ref.at[pl.ds(8 * d, 8)], s0.at[:, pl.ds(at(x), span_y), :]))
    for x in (0, 1, span_x - 2, span_x - 1):
        late.append(copies.start(pot.at[:, x], s0.at[:, pl.ds(at(x), span_y), :]))
    for c in range(8):
        for i, x in enumerate((1, 2, span_x - 3, span_x - 2)):
            s1[c, stored(x), :] = halves[c, kept(i), :]
        for i, x in enumerate((2, 3, span_x - 4, span_x - 3)):
            s2[c, stored(x), :] = nexts[c, kept(i), :]
    for c in range(3):
        rows = pl.ds(3 * span_y, (span_x - 6) * span_y)
        force[c, rows, :] = some_force[c, rows, :]
    for c in range(8):
        for d in range(DEEP):
            p = place(c, d)
            for x in (0, 1, span_x - 2, span_x - 1):
                s0[c, pl.ds(at(x) - 1 - d, 1), :] = nlo[p, pl.ds(x, 1), :]
                s0[c, pl.ds(at(x) + span_y + d, 1), :] = nhi[p, pl.ds(x, 1), :]
    for one in early:
        one.wait()
    for c in range(5):
        for i, x in enumerate((0, 1, 2, span_x - 3, span_x - 2, span_x - 1)):
            field[c, pl.ds(at(x) - 3, span_y + 6), :] = fields[c, pl.ds(i * (ROWS + OFF) + OFF - 3, span_y + 6), :]
    for c in range(12):
        deep = DEEP if c < 8 else FLAT
        ref, part = (s0, c) if c < 8 else (field, c - 8)
        for d in range(deep - 1):
            for e in range(deep - 1 - d):
                p = place(c, d)
                for source, x in ((clo, -1 - e), (chi, span_x + e)):
                    ref[part, pl.ds(at(x) - 1 - d, 1), :] = source[pl.ds(e * 2 * planes + p, 1), :]
                    ref[part, pl.ds(at(x) + span_y + d, 1), :] = source[pl.ds((e * 2 + 1) * planes + p, 1), :]

    def both(low, high, do):
        over(-high, -low, do)
        over(span_x + low, span_x + high, do)

    both(0, 2, lambda x: scale_plane(span_x, span_y, flags, field, x))
    for one in late:
        one.wait()
    both(-1, 2, lambda x: sweep_plane(s0, s1, field, x, 2))
    both(-2, 1, lambda x: sweep_plane(s1, s2, field, x, 1))
    done = [
        copies.start(s2.at[:, pl.ds(at(x), span_y), :], nxt.at[:, x])
        for x in (0, 1, span_x - 2, span_x - 1)
    ]
    both(-3, 0, lambda x: force_plane(s2, field, force, span_y, x))

    table = jnp.concatenate([force[c].astype(BF16) for c in range(3)], axis=1)
    chunk = 256
    upper = lax.broadcasted_iota(jnp.int32, (chunk // 8, 8, depth), 1) < slots
    for i in range(hot.shape[0] // chunk):
        h = hot[pl.ds(i * chunk, chunk), :]
        picked = jnp.dot(h, table, preferred_element_type=F32)
        got = [
            picked[:, c * depth : (c + 1) * depth].reshape(chunk // 8, 8, depth) for c in range(3)
        ]
        both_parts = jnp.concatenate([jnp.where(upper, got[0], got[1]), got[2]], axis=1)
        rows = pl.ds(i * (chunk // 8), chunk // 8)
        sent[rows] = both_parts.astype(BF16)
        one = pltpu.make_async_copy(sent.at[rows], out.at[rows], sent_sems.at[i])
        one.start()
        done.append(one)
    for one in done:
        one.wait()


def flow_kernel(les_x, span_y, vel, wlo, whi, nlo, nhi, base, s0):
    first = 8 * DEEP + 4 * FLAT
    for c in range(3):
        for x in range(les_x):
            s0[c, pl.ds((x + 1) * ROWS + OFF, span_y), :] = vel[c, pl.ds(x * span_y, span_y), :]
        s0[c, pl.ds(OFF, span_y), :] = wlo[first + c]
        s0[c, pl.ds((les_x + 1) * ROWS + OFF, span_y), :] = whi[first + c]
        s0[c, strip(ROWS + OFF - 1, les_x, ROWS), :] = nlo[first + c, pl.ds(0, les_x), :]
        s0[c, strip(ROWS + OFF + span_y, les_x, ROWS), :] = nhi[first + c, pl.ds(0, les_x), :]

    def step(x, carry):
        for t in range(span_y // 8):
            row = (x + 1) * ROWS + OFF + 8 * t
            middle = [s0[c, pl.ds(row, 8), :] for c in range(3)]
            for c in range(3):
                xf = s0[c, pl.ds(row + ROWS, 8), :]
                xb = s0[c, pl.ds(row - ROWS, 8), :]
                yf = s0[c, pl.ds(row + 1, 8), :]
                yb = s0[c, pl.ds(row - 1, 8), :]
                zf, zb = lanes(middle[c])
                carried = 0.5 * (middle[0] * (xf - xb) + middle[1] * (yf - yb) + middle[2] * (zf - zb))
                spread = (xf + xb) + (yf + yb) + (zf + zb) - 6.0 * middle[c]
                base[c, pl.ds(pl.multiple_of(x * span_y + 8 * t, 8), 8), :] = middle[c] + DT * (
                    VISC * spread - carried
                )
        return carry

    lax.fori_loop(0, les_x, step, 0)


def last_kernel(slots, column, got, base, les, nxt):
    lines = base.shape[1]
    depth = got.shape[2]
    wide = got[...].astype(F32)
    values = jnp.concatenate(
        [wide[:, 8 * h : 8 * h + 8, :].reshape(-1, depth).astype(BF16) for h in range(2)], axis=1
    )
    want = column[...]
    lane = lax.broadcasted_iota(jnp.int32, want.shape, 1)
    picked = []
    for half in range(2):
        take = jnp.concatenate(
            [
                jnp.where(want == lane + (depth * k - slots * half), 1.0, 0.0).astype(BF16)
                for k in range(values.shape[0] // depth)
            ],
            axis=1,
        )
        picked.append(jnp.dot(take, values, preferred_element_type=F32))
    for c in range(3):
        push = picked[c % 2][:, (c // 2) * depth : (c // 2 + 1) * depth].astype(BF16)
        les[c] = push
        nxt[c] = base[c] + DT * push.astype(F32)


def call(kernel, out, name, scratch=(), smem=0, count=1, hbm=(), hbm_out=(), alias=None, limit=16):
    vmem = pl.BlockSpec(memory_space=pltpu.VMEM)
    specs = [pl.BlockSpec(memory_space=pltpu.SMEM)] * smem + [vmem] * (count - smem)
    for i in hbm:
        specs[i] = pl.BlockSpec(memory_space=pltpu.HBM)
    return pl.pallas_call(
        kernel,
        out_shape=[jax.ShapeDtypeStruct(shape, kind) for shape, kind in out],
        in_specs=specs,
        out_specs=[
            pl.BlockSpec(memory_space=pltpu.HBM) if i in hbm_out else vmem for i in range(len(out))
        ],
        scratch_shapes=[pltpu.VMEM(*one) if isinstance(one, tuple) else one for one in scratch],
        input_output_aliases=alias or {},
        compiler_params=pltpu.CompilerParams(vmem_limit_bytes=limit * MIB),
        name=name,
    )


def swap(low, high, axis):
    count = lax.axis_size(axis)
    forward = [(i, i + 1) for i in range(count - 1)]
    backward = [(target, source) for source, target in forward]
    return lax.ppermute(high, axis, forward), lax.ppermute(low, axis, backward)


def body(potential, source_current, cell_label, region_kappa, send_lines, recv_slot, velocity):
    _, span_x, span_y, depth = potential.shape
    les_x = velocity.shape[1]
    peers, slots = send_lines.shape[1:]
    regions = region_kappa.shape[0]
    cells = span_x * span_y
    lines = les_x * span_y
    planes = planes_of()
    vel = velocity.reshape(3, lines, depth)

    wide = ((planes, span_y, depth), F32)
    narrow = ((planes, span_x, depth), F32)
    wlo, whi, nlo, nhi = call(
        functools.partial(faces_kernel, span_x, span_y, regions),
        [wide, wide, narrow, narrow],
        "faces",
        scratch=[
            (potential.shape, F32),
            (source_current.shape, F32),
            (cell_label.shape, jnp.int32),
            (velocity.shape, F32),
            pltpu.SemaphoreType.DMA((4,)),
        ],
        smem=1, count=5, hbm=(1, 2, 3, 4), limit=60,
    )(region_kappa, potential, source_current, cell_label, velocity)
    nlo, nhi = swap(nlo, nhi, "narrow")
    wlo, whi = swap(wlo, whi, "wide")

    corner = ((FLAT * 2 * (8 * DEEP + 4 * FLAT), depth), F32)
    clo, chi = call(
        functools.partial(corner_kernel, span_x), [corner, corner], "corner", count=2
    )(nlo, nhi)
    clo, chi = swap(clo, chi, "wide")

    pad = (span_x + 2 * DEEP) * ROWS + OFF
    padded = ((8, pad, depth), F32)
    fields = ((5, pad, depth), F32)
    w, n = lax.axis_index("wide"), lax.axis_index("narrow")
    flags = jnp.stack(
        [w > 0, w < lax.axis_size("wide") - 1, n > 0, n < lax.axis_size("narrow") - 1]
    ).astype(F32)
    keep = ROWS + OFF
    nxt, halves, nexts, edge_fields, force = call(
        functools.partial(inner_kernel, span_x, span_y, regions),
        [
            (potential.shape, F32),
            ((8, 4 * keep, depth), F32),
            ((8, 4 * keep, depth), F32),
            ((5, 6 * keep, depth), F32),
            ((3, cells, depth), F32),
        ],
        "inner",
        scratch=[
            padded,
            padded,
            padded,
            fields,
            ((3, span_x, span_y, depth), F32),
            ((span_x, span_y, depth), jnp.int32),
            pltpu.SemaphoreType.DMA((2 + 2 * span_x,)),
        ],
        smem=2, count=7, hbm=(2, 3, 4), hbm_out=(0,), limit=LIMIT_IN,
    )(flags, region_kappa, potential, source_current, cell_label, nlo, nhi)

    sent = jnp.concatenate([send_lines[0], send_lines[0]], axis=1).reshape(-1)
    hot = (sent[:, None] == jnp.arange(cells, dtype=jnp.int32)[None, :]).astype(BF16)
    potential_next, outgoing = call(
        functools.partial(outer_kernel, span_x, span_y, slots),
        [(potential.shape, F32), ((peers, 16, depth), BF16)],
        "outer",
        scratch=[
            padded,
            padded,
            padded,
            fields,
            ((3, cells, depth), F32),
            ((peers, 16, depth), BF16),
            pltpu.SemaphoreType.DMA((2 * FLAT + 2 * DEEP + 8,)),
            pltpu.SemaphoreType.DMA((hot.shape[0] // 256,)),
        ],
        smem=1, count=14, hbm=(1, 2, 3, 13), hbm_out=(0, 1), alias={13: 0}, limit=LIMIT_OUT,
    )(flags, potential, wlo, whi, nlo, nhi, clo, chi, hot, halves, nexts, edge_fields, force, nxt)

    incoming = lax.all_to_all(
        outgoing, ("wide", "narrow"), split_axis=0, concat_axis=0, tiled=True
    )
    slot = recv_slot[0]
    column = jnp.broadcast_to(((slot // slots) * 8 + slot % slots)[:, None], (lines, 128))
    (base,) = call(
        functools.partial(flow_kernel, les_x, span_y),
        [((3, lines, depth), F32)],
        "flow",
        scratch=[((3, (les_x + 2) * ROWS + OFF, depth), F32)],
        count=5,
    )(vel, wlo, whi, nlo, nhi)
    les, velocity_next = call(
        functools.partial(last_kernel, slots),
        [((3, lines, depth), BF16), ((3, lines, depth), F32)],
        "last", count=3,
    )(column, incoming, base)
    block = (3, les_x, span_y, depth)
    return potential_next, les.reshape(block), velocity_next.reshape(block)


def solution(mesh):
    in_specs = (
        P(None, "wide", "narrow", None),
        P(None, "wide", "narrow", None),
        P("wide", "narrow", None),
        P(),
        P(("wide", "narrow"), None, None),
        P(("wide", "narrow"), None),
        P(None, "wide", "narrow", None),
    )
    out_specs = (
        P(None, "wide", "narrow", None),
        P(None, "wide", "narrow", None),
        P(None, "wide", "narrow", None),
    )
    return jax.shard_map(body, mesh=mesh, in_specs=in_specs, out_specs=out_specs, check_vma=False)
```

```python
import functools

import jax
import jax.numpy as jnp
from jax import lax
from jax.experimental import pallas as pl
from jax.experimental.pallas import tpu as pltpu
from jax.sharding import PartitionSpec as P

DT = 0.25
VISC = 0.5
F32 = jnp.float32
BF16 = jnp.bfloat16
DEEP = 3
FLAT = 2
ROWS = 40
OFF = 8
MIB = 1 << 20
LIMIT_IN = 48
LIMIT_OUT = 48


def strip(start, size, stride):
    return pl.ds(start, size, stride=stride)


def planes_of():
    return 8 * DEEP + 4 * FLAT + 3


def kappa_of(label, rk, regions):
    kappa = jnp.zeros(label.shape, F32)
    for r in range(regions):
        kappa = jnp.where(label == 2 * regions + r, rk[r], kappa)
    return kappa


class Copies:
    def __init__(self, sems):
        self.sems = sems
        self.count = 0

    def start(self, source, target):
        one = pltpu.make_async_copy(source, target, self.sems.at[self.count])
        one.start()
        self.count += 1
        return one


def faces_kernel(
    span_x, span_y, regions, rk, pot, src, lab, vel, wlo, whi, nlo, nhi, all_pot, all_src, all_lab, all_vel, sems
):
    les_x = vel.shape[1]
    flow = 8 * DEEP + 4 * FLAT
    copies = Copies(sems)
    waits = [
        copies.start(source, target)
        for source, target in ((lab, all_lab), (src, all_src), (vel, all_vel), (pot, all_pot))
    ]
    for one in waits[:2]:
        one.wait()
    for side, (wide, narrow) in enumerate(((wlo, nlo), (whi, nhi))):
        for d in range(FLAT):
            x = span_x - FLAT + d if side else d
            y = span_y - 1 - d if side else d
            label = all_lab[x]
            for c in range(3):
                wide[8 * DEEP + 4 * d + c] = jnp.where(label < regions, all_src[c, x], 0.0)
            wide[8 * DEEP + 4 * d + 3] = kappa_of(label, rk, regions)
            label = all_lab[:, y, :]
            for c in range(3):
                narrow[8 * DEEP + 4 * d + c] = jnp.where(label < regions, all_src[c, :, y, :], 0.0)
            narrow[8 * DEEP + 4 * d + 3] = kappa_of(label, rk, regions)
    waits[2].wait()
    for side, (wide, narrow) in enumerate(((wlo, nlo), (whi, nhi))):
        for c in range(3):
            wide[flow + c] = all_vel[c, side * (les_x - 1)]
            narrow[flow + c, pl.ds(0, les_x), :] = all_vel[c, :, side * (span_y - 1), :]
            narrow[flow + c, pl.ds(les_x, span_x - les_x), :] = jnp.zeros((span_x - les_x, vel.shape[3]), F32)
    waits[3].wait()
    for side, (wide, narrow) in enumerate(((wlo, nlo), (whi, nhi))):
        for d in range(DEEP):
            x = span_x - DEEP + d if side else d
            y = span_y - 1 - d if side else d
            for c in range(8):
                wide[8 * d + c] = all_pot[c, x]
                narrow[8 * d + c] = all_pot[c, :, y, :]


def corner_kernel(span_x, nlo, nhi, clo, chi):
    planes = 8 * DEEP + 4 * FLAT
    for d in range(FLAT):
        for side, ref in enumerate((nlo, nhi)):
            rows = pl.ds((d * 2 + side) * planes, planes)
            clo[rows, :] = ref[:planes, d, :]
            chi[rows, :] = ref[:planes, span_x - 1 - d, :]


def place(c, d):
    return 8 * d + c if c < 8 else 8 * DEEP + 4 * d + c - 8


def at(x):
    return (x + DEEP) * ROWS + OFF


def scale_plane(span_x, span_y, flags, field, x):
    line = lax.broadcasted_iota(jnp.int32, (8, field.shape[-1]), 0)
    fx = jnp.where(x < 0, flags[0], jnp.where(x >= span_x, flags[1], 1.0))
    for t in range(5):
        row = at(x) - FLAT + 8 * t
        y = line + (8 * t - FLAT)
        fy = jnp.where(y < 0, flags[2], jnp.where(y >= span_y, flags[3], 1.0))
        kappa = field[3, pl.ds(row, 8), :]
        field[4, pl.ds(row, 8), :] = (fx * fy) / (36.0 + kappa * kappa)


def sweep_plane(old, new, field, x, margin):
    for t in range(5):
        sweep_tile(old, new, field, at(x) - margin + 8 * t)


def over(low, high, do):
    def step(i, carry):
        do(i + low)
        return carry

    lax.fori_loop(0, high - low, step, 0)


def lanes(value):
    depth = value.shape[-1]
    lane = lax.broadcasted_iota(jnp.int32, value.shape, 1)
    ahead = jnp.where(lane == depth - 1, 0.0, pltpu.roll(value, depth - 1, 1))
    back = jnp.where(lane == 0, 0.0, pltpu.roll(value, 1, 1))
    return ahead, back


def sweep_tile(old, new, field, row):
    s6 = 6.0 * field[4, pl.ds(row, 8), :]
    kappa = field[3, pl.ds(row, 8), :]
    sk = kappa * field[4, pl.ds(row, 8), :]
    half = 0.5 * kappa
    total = []
    diff = []
    for c in range(8):
        xf = old[c, pl.ds(row + ROWS, 8), :]
        xb = old[c, pl.ds(row - ROWS, 8), :]
        yf = old[c, pl.ds(row + 1, 8), :]
        yb = old[c, pl.ds(row - 1, 8), :]
        zf, zb = lanes(old[c, pl.ds(row, 8), :])
        total.append((xf + xb) + (yf + yb) + (zf + zb))
        if c % 4 == 3:
            diff.append((xf - xb, yf - yb, zf - zb))
        else:
            diff.append(((xf - xb), (yf - yb), (zf - zb))[c % 4])
    for c in range(3):
        first = (field[c, pl.ds(row, 8), :] + total[c]) + half * diff[7][c]
        second = total[4 + c] - half * diff[3][c]
        new[c, pl.ds(row, 8), :] = s6 * first + sk * second
        new[4 + c, pl.ds(row, 8), :] = s6 * second - sk * first
    first = total[3] + half * (diff[4] + diff[5] + diff[6])
    second = total[7] - half * (diff[0] + diff[1] + diff[2])
    new[3, pl.ds(row, 8), :] = s6 * first + sk * second
    new[7, pl.ds(row, 8), :] = s6 * second - sk * first


def lorentz_tile(now, field, row):
    def grab(c, shift):
        return now[c, pl.ds(row + shift, 8), :]

    kappa = field[3, pl.ds(row, 8), :]

    def part(base):
        a = [grab(base + c, 0) for c in range(3)]
        azf, azb = lanes(a[0])
        bzf, bzb = lanes(a[1])
        curl = [
            (grab(base + 2, 1) - grab(base + 2, -1)) - (bzf - bzb),
            (azf - azb) - (grab(base + 2, ROWS) - grab(base + 2, -ROWS)),
            (grab(base + 1, ROWS) - grab(base + 1, -ROWS)) - (grab(base, 1) - grab(base, -1)),
        ]
        phi = grab(base + 3, 0)
        pzf, pzb = lanes(phi)
        grad = [
            grab(base + 3, ROWS) - grab(base + 3, -ROWS),
            grab(base + 3, 1) - grab(base + 3, -1),
            pzf - pzb,
        ]
        return curl, [a[c] + 0.5 * grad[c] for c in range(3)]

    real_b, field_re = part(0)
    imag_b, field_im = part(4)
    cur_re = [field[c, pl.ds(row, 8), :] + kappa * field_im[c] for c in range(3)]
    cur_im = [-kappa * field_re[c] for c in range(3)]
    force = []
    for c in range(3):
        n = (c + 1) % 3
        f = (c + 2) % 3
        value = (cur_re[n] * real_b[f] - cur_re[f] * real_b[n]) + (
            cur_im[n] * imag_b[f] - cur_im[f] * imag_b[n]
        )
        force.append(jnp.where(kappa > 0.0, 0.25 * value, 0.0))
    return force


def force_plane(now, field, force, span_y, x):
    for t in range(span_y // 8):
        f = lorentz_tile(now, field, at(x) + 8 * t)
        rows = pl.ds(pl.multiple_of(x * span_y + 8 * t, 8), 8)
        for c in range(3):
            force[c, rows, :] = f[c]


def stored(x):
    return pl.ds((x + DEEP) * ROWS, ROWS + OFF)


def kept(i):
    return pl.ds(i * (ROWS + OFF), ROWS + OFF)


def inner_kernel(
    span_x, span_y, regions, flags, rk, pot, src, lab, nlo, nhi,
    nxt, halves, nexts, fields, force, s0, s1, s2, field, some, tags, sems,
):
    copies = Copies(sems)
    early = [copies.start(lab, tags), copies.start(src, some)]
    late = [
        copies.start(pot.at[:, x], s0.at[:, pl.ds(at(x), span_y), :]) for x in range(span_x)
    ]
    for c in range(12):
        deep = DEEP if c < 8 else FLAT
        ref, part = (s0, c) if c < 8 else (field, c - 8)
        for d in range(deep):
            ref[part, strip(at(0) - 1 - d, span_x, ROWS), :] = nlo[place(c, d)] * flags[2]
            ref[part, strip(at(0) + span_y + d, span_x, ROWS), :] = nhi[place(c, d)] * flags[3]
    for one in early:
        one.wait()

    def lay(x):
        there = pl.ds(pl.multiple_of((x + DEEP) * ROWS + OFF, 8), span_y)
        label = tags[x]
        for c in range(3):
            field[c, there, :] = jnp.where(label < regions, some[c, x], 0.0)
        field[3, there, :] = kappa_of(label, rk, regions)

    over(0, span_x, lay)
    over(0, span_x, lambda x: scale_plane(span_x, span_y, flags, field, x))
    for one in late:
        one.wait()
    over(1, span_x - 1, lambda x: sweep_plane(s0, s1, field, x, 2))
    over(2, span_x - 2, lambda x: sweep_plane(s1, s2, field, x, 1))
    done = [
        copies.start(s2.at[:, pl.ds(at(x), span_y), :], nxt.at[:, x]) for x in range(2, span_x - 2)
    ]
    over(3, span_x - 3, lambda x: force_plane(s2, field, force, span_y, x))
    for c in range(8):
        for i, x in enumerate((1, 2, span_x - 3, span_x - 2)):
            halves[c, kept(i), :] = s1[c, stored(x), :]
        for i, x in enumerate((2, 3, span_x - 4, span_x - 3)):
            nexts[c, kept(i), :] = s2[c, stored(x), :]
    for c in range(5):
        for i, x in enumerate((0, 1, 2, span_x - 3, span_x - 2, span_x - 1)):
            fields[c, kept(i), :] = field[c, stored(x), :]
    for one in done:
        one.wait()


def outer_kernel(
    span_x, span_y, slots, flags, pot, wlo, whi, nlo, nhi, clo, chi, hot, halves, nexts, fields, some_force, old_nxt,
    nxt, out, s0, s1, s2, field, force, sent, sems, sent_sems,
):
    depth = pot.shape[-1]
    planes = 8 * DEEP + 4 * FLAT
    copies = Copies(sems)
    early = []
    late = []
    for d in range(FLAT):
        for ref, x in ((wlo, d - FLAT), (whi, span_x + d)):
            early.append(
                copies.start(ref.at[pl.ds(8 * DEEP + 4 * d, 4)], field.at[pl.ds(0, 4), pl.ds(at(x), span_y), :])
            )
    for d in range(DEEP):
        for ref, x in ((wlo, d - DEEP), (whi, span_x + d)):
            late.append(copies.start(ref.at[pl.ds(8 * d, 8)], s0.at[:, pl.ds(at(x), span_y), :]))
    for x in (0, 1, span_x - 2, span_x - 1):
        late.append(copies.start(pot.at[:, x], s0.at[:, pl.ds(at(x), span_y), :]))
    for c in range(8):
        for i, x in enumerate((1, 2, span_x - 3, span_x - 2)):
            s1[c, stored(x), :] = halves[c, kept(i), :]
        for i, x in enumerate((2, 3, span_x - 4, span_x - 3)):
            s2[c, stored(x), :] = nexts[c, kept(i), :]
    for c in range(3):
        rows = pl.ds(3 * span_y, (span_x - 6) * span_y)
        force[c, rows, :] = some_force[c, rows, :]
    for c in range(8):
        for d in range(DEEP):
            p = place(c, d)
            for x in (0, 1, span_x - 2, span_x - 1):
                s0[c, pl.ds(at(x) - 1 - d, 1), :] = nlo[p, pl.ds(x, 1), :] * flags[2]
                s0[c, pl.ds(at(x) + span_y + d, 1), :] = nhi[p, pl.ds(x, 1), :] * flags[3]
    for one in early:
        one.wait()
    for c in range(5):
        for i, x in enumerate((0, 1, 2, span_x - 3, span_x - 2, span_x - 1)):
            field[c, pl.ds(at(x) - 3, span_y + 6), :] = fields[c, pl.ds(i * (ROWS + OFF) + OFF - 3, span_y + 6), :]
    for c in range(12):
        deep = DEEP if c < 8 else FLAT
        ref, part = (s0, c) if c < 8 else (field, c - 8)
        for d in range(deep - 1):
            for e in range(deep - 1 - d):
                p = place(c, d)
                for source, x in ((clo, -1 - e), (chi, span_x + e)):
                    low, high = (source[pl.ds((e * 2 + side) * planes + p, 1), :] for side in range(2))
                    ref[part, pl.ds(at(x) - 1 - d, 1), :] = low * flags[2]
                    ref[part, pl.ds(at(x) + span_y + d, 1), :] = high * flags[3]

    def both(low, high, do):
        over(-high, -low, do)
        over(span_x + low, span_x + high, do)

    both(0, 2, lambda x: scale_plane(span_x, span_y, flags, field, x))
    for one in late:
        one.wait()
    for i, first in enumerate((-DEEP, span_x)):

        @pl.when(flags[i] == 0.0)
        def _():
            for c in range(8):
                for x in range(first, first + DEEP):
                    s0[c, pl.ds(at(x) - DEEP, span_y + 2 * DEEP), :] = jnp.zeros((span_y + 2 * DEEP, depth), F32)

    both(-1, 2, lambda x: sweep_plane(s0, s1, field, x, 2))
    both(-2, 1, lambda x: sweep_plane(s1, s2, field, x, 1))
    done = [
        copies.start(s2.at[:, pl.ds(at(x), span_y), :], nxt.at[:, x])
        for x in (0, 1, span_x - 2, span_x - 1)
    ]
    both(-3, 0, lambda x: force_plane(s2, field, force, span_y, x))

    table = jnp.concatenate([force[c].astype(BF16) for c in range(3)], axis=1)
    chunk = 256
    upper = lax.broadcasted_iota(jnp.int32, (chunk // 8, 8, depth), 1) < slots
    for i in range(hot.shape[0] // chunk):
        h = hot[pl.ds(i * chunk, chunk), :]
        picked = jnp.dot(h, table, preferred_element_type=F32)
        got = [
            picked[:, c * depth : (c + 1) * depth].reshape(chunk // 8, 8, depth) for c in range(3)
        ]
        both_parts = jnp.concatenate([jnp.where(upper, got[0], got[1]), got[2]], axis=1)
        rows = pl.ds(i * (chunk // 8), chunk // 8)
        sent[rows] = both_parts.astype(BF16)
        one = pltpu.make_async_copy(sent.at[rows], out.at[rows], sent_sems.at[i])
        one.start()
        done.append(one)
    for one in done:
        one.wait()


def flow_kernel(les_x, span_y, flags, vel, wlo, whi, nlo, nhi, base, s0):
    first = 8 * DEEP + 4 * FLAT
    for c in range(3):
        for x in range(les_x):
            s0[c, pl.ds((x + 1) * ROWS + OFF, span_y), :] = vel[c, pl.ds(x * span_y, span_y), :]
        s0[c, pl.ds(OFF, span_y), :] = wlo[first + c] * flags[0]
        s0[c, pl.ds((les_x + 1) * ROWS + OFF, span_y), :] = whi[first + c] * flags[1]
        s0[c, strip(ROWS + OFF - 1, les_x, ROWS), :] = nlo[first + c, pl.ds(0, les_x), :] * flags[2]
        s0[c, strip(ROWS + OFF + span_y, les_x, ROWS), :] = nhi[first + c, pl.ds(0, les_x), :] * flags[3]

    def step(x, carry):
        for t in range(span_y // 8):
            row = (x + 1) * ROWS + OFF + 8 * t
            middle = [s0[c, pl.ds(row, 8), :] for c in range(3)]
            for c in range(3):
                xf = s0[c, pl.ds(row + ROWS, 8), :]
                xb = s0[c, pl.ds(row - ROWS, 8), :]
                yf = s0[c, pl.ds(row + 1, 8), :]
                yb = s0[c, pl.ds(row - 1, 8), :]
                zf, zb = lanes(middle[c])
                carried = 0.5 * (middle[0] * (xf - xb) + middle[1] * (yf - yb) + middle[2] * (zf - zb))
                spread = (xf + xb) + (yf + yb) + (zf + zb) - 6.0 * middle[c]
                base[c, pl.ds(pl.multiple_of(x * span_y + 8 * t, 8), 8), :] = middle[c] + DT * (
                    VISC * spread - carried
                )
        return carry

    lax.fori_loop(0, les_x, step, 0)


def last_kernel(slots, column, got, base, les, nxt):
    lines = base.shape[1]
    depth = got.shape[2]
    wide = got[...].astype(F32)
    values = jnp.concatenate(
        [wide[:, 8 * h : 8 * h + 8, :].reshape(-1, depth).astype(BF16) for h in range(2)], axis=1
    )
    want = column[...]
    lane = lax.broadcasted_iota(jnp.int32, want.shape, 1)
    picked = []
    for half in range(2):
        take = jnp.concatenate(
            [
                jnp.where(want == lane + (depth * k - slots * half), 1.0, 0.0).astype(BF16)
                for k in range(values.shape[0] // depth)
            ],
            axis=1,
        )
        picked.append(jnp.dot(take, values, preferred_element_type=F32))
    for c in range(3):
        push = picked[c % 2][:, (c // 2) * depth : (c // 2 + 1) * depth].astype(BF16)
        les[c] = push
        nxt[c] = base[c] + DT * push.astype(F32)


def call(kernel, out, name, scratch=(), smem=0, count=1, hbm=(), hbm_out=(), alias=None, limit=16):
    vmem = pl.BlockSpec(memory_space=pltpu.VMEM)
    specs = [pl.BlockSpec(memory_space=pltpu.SMEM)] * smem + [vmem] * (count - smem)
    for i in hbm:
        specs[i] = pl.BlockSpec(memory_space=pltpu.HBM)
    return pl.pallas_call(
        kernel,
        out_shape=[jax.ShapeDtypeStruct(shape, kind) for shape, kind in out],
        in_specs=specs,
        out_specs=[
            pl.BlockSpec(memory_space=pltpu.HBM) if i in hbm_out else vmem for i in range(len(out))
        ],
        scratch_shapes=[pltpu.VMEM(*one) if isinstance(one, tuple) else one for one in scratch],
        input_output_aliases=alias or {},
        compiler_params=pltpu.CompilerParams(vmem_limit_bytes=limit * MIB),
        name=name,
    )


def swap(low, high, axis):
    count = lax.axis_size(axis)
    forward = [(i, (i + 1) % count) for i in range(count)]
    backward = [(target, source) for source, target in forward]
    return lax.ppermute(high, axis, forward), lax.ppermute(low, axis, backward)


def body(potential, source_current, cell_label, region_kappa, send_lines, recv_slot, velocity):
    _, span_x, span_y, depth = potential.shape
    les_x = velocity.shape[1]
    peers, slots = send_lines.shape[1:]
    regions = region_kappa.shape[0]
    cells = span_x * span_y
    lines = les_x * span_y
    planes = planes_of()
    vel = velocity.reshape(3, lines, depth)

    wide = ((planes, span_y, depth), F32)
    narrow = ((planes, span_x, depth), F32)
    wlo, whi, nlo, nhi = call(
        functools.partial(faces_kernel, span_x, span_y, regions),
        [wide, wide, narrow, narrow],
        "faces",
        scratch=[
            (potential.shape, F32),
            (source_current.shape, F32),
            (cell_label.shape, jnp.int32),
            (velocity.shape, F32),
            pltpu.SemaphoreType.DMA((4,)),
        ],
        smem=1, count=5, hbm=(1, 2, 3, 4), limit=60,
    )(region_kappa, potential, source_current, cell_label, velocity)
    nlo, nhi = swap(nlo, nhi, "narrow")
    wlo, whi = swap(wlo, whi, "wide")

    corner = ((FLAT * 2 * (8 * DEEP + 4 * FLAT), depth), F32)
    clo, chi = call(
        functools.partial(corner_kernel, span_x), [corner, corner], "corner", count=2
    )(nlo, nhi)
    clo, chi = swap(clo, chi, "wide")

    pad = (span_x + 2 * DEEP) * ROWS + OFF
    padded = ((8, pad, depth), F32)
    fields = ((5, pad, depth), F32)
    w, n = lax.axis_index("wide"), lax.axis_index("narrow")
    flags = jnp.stack(
        [w > 0, w < lax.axis_size("wide") - 1, n > 0, n < lax.axis_size("narrow") - 1]
    ).astype(F32)
    keep = ROWS + OFF
    nxt, halves, nexts, edge_fields, force = call(
        functools.partial(inner_kernel, span_x, span_y, regions),
        [
            (potential.shape, F32),
            ((8, 4 * keep, depth), F32),
            ((8, 4 * keep, depth), F32),
            ((5, 6 * keep, depth), F32),
            ((3, cells, depth), F32),
        ],
        "inner",
        scratch=[
            padded,
            padded,
            padded,
            fields,
            ((3, span_x, span_y, depth), F32),
            ((span_x, span_y, depth), jnp.int32),
            pltpu.SemaphoreType.DMA((2 + 2 * span_x,)),
        ],
        smem=2, count=7, hbm=(2, 3, 4), hbm_out=(0,), limit=LIMIT_IN,
    )(flags, region_kappa, potential, source_current, cell_label, nlo, nhi)

    sent = jnp.concatenate([send_lines[0], send_lines[0]], axis=1).reshape(-1)
    hot = (sent[:, None] == jnp.arange(cells, dtype=jnp.int32)[None, :]).astype(BF16)
    potential_next, outgoing = call(
        functools.partial(outer_kernel, span_x, span_y, slots),
        [(potential.shape, F32), ((peers, 16, depth), BF16)],
        "outer",
        scratch=[
            padded,
            padded,
            padded,
            fields,
            ((3, cells, depth), F32),
            ((peers, 16, depth), BF16),
            pltpu.SemaphoreType.DMA((2 * FLAT + 2 * DEEP + 8,)),
            pltpu.SemaphoreType.DMA((hot.shape[0] // 256,)),
        ],
        smem=1, count=14, hbm=(1, 2, 3, 13), hbm_out=(0, 1), alias={13: 0}, limit=LIMIT_OUT,
    )(flags, potential, wlo, whi, nlo, nhi, clo, chi, hot, halves, nexts, edge_fields, force, nxt)

    incoming = lax.all_to_all(
        outgoing, ("wide", "narrow"), split_axis=0, concat_axis=0, tiled=True
    )
    slot = recv_slot[0]
    column = jnp.broadcast_to(((slot // slots) * 8 + slot % slots)[:, None], (lines, 128))
    (base,) = call(
        functools.partial(flow_kernel, les_x, span_y),
        [((3, lines, depth), F32)],
        "flow",
        scratch=[((3, (les_x + 2) * ROWS + OFF, depth), F32)],
        smem=1, count=6,
    )(flags, vel, wlo, whi, nlo, nhi)
    les, velocity_next = call(
        functools.partial(last_kernel, slots),
        [((3, lines, depth), BF16), ((3, lines, depth), F32)],
        "last", count=3,
    )(column, incoming, base)
    block = (3, les_x, span_y, depth)
    return potential_next, les.reshape(block), velocity_next.reshape(block)


def solution(mesh):
    in_specs = (
        P(None, "wide", "narrow", None),
        P(None, "wide", "narrow", None),
        P("wide", "narrow", None),
        P(),
        P(("wide", "narrow"), None, None),
        P(("wide", "narrow"), None),
        P(None, "wide", "narrow", None),
    )
    out_specs = (
        P(None, "wide", "narrow", None),
        P(None, "wide", "narrow", None),
        P(None, "wide", "narrow", None),
    )
    return jax.shard_map(body, mesh=mesh, in_specs=in_specs, out_specs=out_specs, check_vma=False)
```

```python
import functools

import jax
import jax.numpy as jnp
from jax import lax
from jax.experimental import pallas as pl
from jax.experimental.pallas import tpu as pltpu
from jax.sharding import PartitionSpec as P

DT = 0.25
VISC = 0.5
F32 = jnp.float32
BF16 = jnp.bfloat16
DEEP = 3
FLAT = 2
ROWS = 40
OFF = 8
MIB = 1 << 20
LIMIT_IN = 48
LIMIT_OUT = 48


def strip(start, size, stride):
    return pl.ds(start, size, stride=stride)


def planes_of():
    return 8 * DEEP + 4 * FLAT + 3


def kappa_of(label, rk, regions):
    kappa = jnp.zeros(label.shape, F32)
    for r in range(regions):
        kappa = jnp.where(label == 2 * regions + r, rk[r], kappa)
    return kappa


class Copies:
    def __init__(self, sems):
        self.sems = sems
        self.count = 0

    def start(self, source, target):
        one = pltpu.make_async_copy(source, target, self.sems.at[self.count])
        one.start()
        self.count += 1
        return one


def faces_kernel(
    span_x, span_y, regions, rk, pot, src, lab, vel, wlo, whi, nlo, nhi, all_pot, all_src, all_lab, all_vel, sems
):
    les_x = vel.shape[1]
    flow = 8 * DEEP + 4 * FLAT
    copies = Copies(sems)
    waits = [
        copies.start(source, target)
        for source, target in ((lab, all_lab), (src, all_src), (vel, all_vel), (pot, all_pot))
    ]
    for one in waits[:2]:
        one.wait()
    for side, (wide, narrow) in enumerate(((wlo, nlo), (whi, nhi))):
        for d in range(FLAT):
            x = span_x - FLAT + d if side else d
            y = span_y - 1 - d if side else d
            label = all_lab[x]
            for c in range(3):
                wide[8 * DEEP + 4 * d + c] = jnp.where(label < regions, all_src[c, x], 0.0)
            wide[8 * DEEP + 4 * d + 3] = kappa_of(label, rk, regions)
            label = all_lab[:, y, :]
            for c in range(3):
                narrow[8 * DEEP + 4 * d + c] = jnp.where(label < regions, all_src[c, :, y, :], 0.0)
            narrow[8 * DEEP + 4 * d + 3] = kappa_of(label, rk, regions)
    waits[2].wait()
    for side, (wide, narrow) in enumerate(((wlo, nlo), (whi, nhi))):
        for c in range(3):
            wide[flow + c] = all_vel[c, side * (les_x - 1)]
            narrow[flow + c, pl.ds(0, les_x), :] = all_vel[c, :, side * (span_y - 1), :]
            narrow[flow + c, pl.ds(les_x, span_x - les_x), :] = jnp.zeros((span_x - les_x, vel.shape[3]), F32)
    waits[3].wait()
    for side, (wide, narrow) in enumerate(((wlo, nlo), (whi, nhi))):
        for d in range(DEEP):
            x = span_x - DEEP + d if side else d
            y = span_y - 1 - d if side else d
            for c in range(8):
                wide[8 * d + c] = all_pot[c, x]
                narrow[8 * d + c] = all_pot[c, :, y, :]


def corner_kernel(span_x, nlo, nhi, clo, chi):
    planes = 8 * DEEP + 4 * FLAT
    for d in range(FLAT):
        for side, ref in enumerate((nlo, nhi)):
            rows = pl.ds((d * 2 + side) * planes, planes)
            clo[rows, :] = ref[:planes, d, :]
            chi[rows, :] = ref[:planes, span_x - 1 - d, :]


def place(c, d):
    return 8 * d + c if c < 8 else 8 * DEEP + 4 * d + c - 8


def at(x):
    return (x + DEEP) * ROWS + OFF


def scale_plane(span_x, span_y, flags, field, x):
    line = lax.broadcasted_iota(jnp.int32, (8, field.shape[-1]), 0)
    fx = jnp.where(x < 0, flags[0], jnp.where(x >= span_x, flags[1], 1.0))
    for t in range(5):
        row = at(x) - FLAT + 8 * t
        y = line + (8 * t - FLAT)
        fy = jnp.where(y < 0, flags[2], jnp.where(y >= span_y, flags[3], 1.0))
        kappa = field[3, pl.ds(row, 8), :]
        field[4, pl.ds(row, 8), :] = (fx * fy) / (36.0 + kappa * kappa)


def sweep_plane(old, new, field, x, margin):
    for t in range(5):
        sweep_tile(old, new, field, at(x) - margin + 8 * t)


def over(low, high, do, unroll=1):
    def step(i, carry):
        do(i + low)
        return carry

    lax.fori_loop(0, high - low, step, 0, unroll=unroll)


def lanes(value):
    depth = value.shape[-1]
    lane = lax.broadcasted_iota(jnp.int32, value.shape, 1)
    ahead = jnp.where(lane == depth - 1, 0.0, pltpu.roll(value, depth - 1, 1))
    back = jnp.where(lane == 0, 0.0, pltpu.roll(value, 1, 1))
    return ahead, back


def sweep_tile(old, new, field, row):
    s6 = 6.0 * field[4, pl.ds(row, 8), :]
    kappa = field[3, pl.ds(row, 8), :]
    sk = kappa * field[4, pl.ds(row, 8), :]
    half = 0.5 * kappa
    total = []
    diff = []
    for c in range(8):
        xf = old[c, pl.ds(row + ROWS, 8), :]
        xb = old[c, pl.ds(row - ROWS, 8), :]
        yf = old[c, pl.ds(row + 1, 8), :]
        yb = old[c, pl.ds(row - 1, 8), :]
        zf, zb = lanes(old[c, pl.ds(row, 8), :])
        total.append((xf + xb) + (yf + yb) + (zf + zb))
        if c % 4 == 3:
            diff.append((xf - xb, yf - yb, zf - zb))
        else:
            diff.append(((xf - xb), (yf - yb), (zf - zb))[c % 4])
    for c in range(3):
        first = (field[c, pl.ds(row, 8), :] + total[c]) + half * diff[7][c]
        second = total[4 + c] - half * diff[3][c]
        new[c, pl.ds(row, 8), :] = s6 * first + sk * second
        new[4 + c, pl.ds(row, 8), :] = s6 * second - sk * first
    first = total[3] + half * (diff[4] + diff[5] + diff[6])
    second = total[7] - half * (diff[0] + diff[1] + diff[2])
    new[3, pl.ds(row, 8), :] = s6 * first + sk * second
    new[7, pl.ds(row, 8), :] = s6 * second - sk * first


def lorentz_tile(now, field, row):
    def grab(c, shift):
        return now[c, pl.ds(row + shift, 8), :]

    kappa = field[3, pl.ds(row, 8), :]

    def part(base):
        a = [grab(base + c, 0) for c in range(3)]
        azf, azb = lanes(a[0])
        bzf, bzb = lanes(a[1])
        curl = [
            (grab(base + 2, 1) - grab(base + 2, -1)) - (bzf - bzb),
            (azf - azb) - (grab(base + 2, ROWS) - grab(base + 2, -ROWS)),
            (grab(base + 1, ROWS) - grab(base + 1, -ROWS)) - (grab(base, 1) - grab(base, -1)),
        ]
        phi = grab(base + 3, 0)
        pzf, pzb = lanes(phi)
        grad = [
            grab(base + 3, ROWS) - grab(base + 3, -ROWS),
            grab(base + 3, 1) - grab(base + 3, -1),
            pzf - pzb,
        ]
        return curl, [a[c] + 0.5 * grad[c] for c in range(3)]

    real_b, field_re = part(0)
    imag_b, field_im = part(4)
    cur_re = [field[c, pl.ds(row, 8), :] + kappa * field_im[c] for c in range(3)]
    cur_im = [-kappa * field_re[c] for c in range(3)]
    force = []
    for c in range(3):
        n = (c + 1) % 3
        f = (c + 2) % 3
        value = (cur_re[n] * real_b[f] - cur_re[f] * real_b[n]) + (
            cur_im[n] * imag_b[f] - cur_im[f] * imag_b[n]
        )
        force.append(jnp.where(kappa > 0.0, 0.25 * value, 0.0))
    return force


def force_plane(now, field, force, span_y, x):
    for t in range(span_y // 8):
        f = lorentz_tile(now, field, at(x) + 8 * t)
        rows = pl.ds(pl.multiple_of(x * span_y + 8 * t, 8), 8)
        for c in range(3):
            force[c, rows, :] = f[c]


def stored(x):
    return pl.ds((x + DEEP) * ROWS, ROWS + OFF)


def kept(i):
    return pl.ds(i * (ROWS + OFF), ROWS + OFF)


def inner_kernel(
    span_x, span_y, regions, flags, rk, pot, src, lab, nlo, nhi,
    nxt, halves, nexts, fields, force, s0, s1, s2, field, some, tags, sems,
):
    copies = Copies(sems)
    early = [copies.start(lab, tags), copies.start(src, some)]
    late = [
        copies.start(pot.at[:, x], s0.at[:, pl.ds(at(x), span_y), :]) for x in range(span_x)
    ]
    for c in range(12):
        deep = DEEP if c < 8 else FLAT
        ref, part = (s0, c) if c < 8 else (field, c - 8)
        for d in range(deep):
            ref[part, strip(at(0) - 1 - d, span_x, ROWS), :] = nlo[place(c, d)] * flags[2]
            ref[part, strip(at(0) + span_y + d, span_x, ROWS), :] = nhi[place(c, d)] * flags[3]
    for one in early:
        one.wait()

    def lay(x):
        there = pl.ds(pl.multiple_of((x + DEEP) * ROWS + OFF, 8), span_y)
        label = tags[x]
        for c in range(3):
            field[c, there, :] = jnp.where(label < regions, some[c, x], 0.0)
        field[3, there, :] = kappa_of(label, rk, regions)

    over(0, span_x, lay)
    over(0, span_x, lambda x: scale_plane(span_x, span_y, flags, field, x))
    for one in late:
        one.wait()
    over(1, span_x - 1, lambda x: sweep_plane(s0, s1, field, x, 2), 7)
    over(2, span_x - 2, lambda x: sweep_plane(s1, s2, field, x, 1), 7)
    done = [
        copies.start(s2.at[:, pl.ds(at(x), span_y), :], nxt.at[:, x]) for x in range(2, span_x - 2)
    ]
    over(3, span_x - 3, lambda x: force_plane(s2, field, force, span_y, x), 5)
    for c in range(8):
        for i, x in enumerate((1, 2, span_x - 3, span_x - 2)):
            halves[c, kept(i), :] = s1[c, stored(x), :]
        for i, x in enumerate((2, 3, span_x - 4, span_x - 3)):
            nexts[c, kept(i), :] = s2[c, stored(x), :]
    for c in range(5):
        for i, x in enumerate((0, 1, 2, span_x - 3, span_x - 2, span_x - 1)):
            fields[c, kept(i), :] = field[c, stored(x), :]
    for one in done:
        one.wait()


def outer_kernel(
    span_x, span_y, slots, flags, pot, wlo, whi, nlo, nhi, clo, chi, hot, halves, nexts, fields, some_force, old_nxt,
    nxt, out, s0, s1, s2, field, force, sent, sems, sent_sems,
):
    depth = pot.shape[-1]
    planes = 8 * DEEP + 4 * FLAT
    copies = Copies(sems)
    early = []
    late = []
    for d in range(FLAT):
        for ref, x in ((wlo, d - FLAT), (whi, span_x + d)):
            early.append(
                copies.start(ref.at[pl.ds(8 * DEEP + 4 * d, 4)], field.at[pl.ds(0, 4), pl.ds(at(x), span_y), :])
            )
    for d in range(DEEP):
        for ref, x in ((wlo, d - DEEP), (whi, span_x + d)):
            late.append(copies.start(ref.at[pl.ds(8 * d, 8)], s0.at[:, pl.ds(at(x), span_y), :]))
    for x in (0, 1, span_x - 2, span_x - 1):
        late.append(copies.start(pot.at[:, x], s0.at[:, pl.ds(at(x), span_y), :]))
    for c in range(8):
        for i, x in enumerate((1, 2, span_x - 3, span_x - 2)):
            s1[c, stored(x), :] = halves[c, kept(i), :]
        for i, x in enumerate((2, 3, span_x - 4, span_x - 3)):
            s2[c, stored(x), :] = nexts[c, kept(i), :]
    for c in range(3):
        rows = pl.ds(3 * span_y, (span_x - 6) * span_y)
        force[c, rows, :] = some_force[c, rows, :]
    for c in range(8):
        for d in range(DEEP):
            p = place(c, d)
            for x in (0, 1, span_x - 2, span_x - 1):
                s0[c, pl.ds(at(x) - 1 - d, 1), :] = nlo[p, pl.ds(x, 1), :] * flags[2]
                s0[c, pl.ds(at(x) + span_y + d, 1), :] = nhi[p, pl.ds(x, 1), :] * flags[3]
    for one in early:
        one.wait()
    for c in range(5):
        for i, x in enumerate((0, 1, 2, span_x - 3, span_x - 2, span_x - 1)):
            field[c, pl.ds(at(x) - 3, span_y + 6), :] = fields[c, pl.ds(i * (ROWS + OFF) + OFF - 3, span_y + 6), :]
    for c in range(12):
        deep = DEEP if c < 8 else FLAT
        ref, part = (s0, c) if c < 8 else (field, c - 8)
        for d in range(deep - 1):
            for e in range(deep - 1 - d):
                p = place(c, d)
                for source, x in ((clo, -1 - e), (chi, span_x + e)):
                    low, high = (source[pl.ds((e * 2 + side) * planes + p, 1), :] for side in range(2))
                    ref[part, pl.ds(at(x) - 1 - d, 1), :] = low * flags[2]
                    ref[part, pl.ds(at(x) + span_y + d, 1), :] = high * flags[3]

    def both(low, high, do):
        over(-high, -low, do, 3)
        over(span_x + low, span_x + high, do, 3)

    both(0, 2, lambda x: scale_plane(span_x, span_y, flags, field, x))
    for one in late:
        one.wait()
    for i, first in enumerate((-DEEP, span_x)):

        @pl.when(flags[i] == 0.0)
        def _():
            for c in range(8):
                for x in range(first, first + DEEP):
                    s0[c, pl.ds(at(x) - DEEP, span_y + 2 * DEEP), :] = jnp.zeros((span_y + 2 * DEEP, depth), F32)

    both(-1, 2, lambda x: sweep_plane(s0, s1, field, x, 2))
    both(-2, 1, lambda x: sweep_plane(s1, s2, field, x, 1))
    done = [
        copies.start(s2.at[:, pl.ds(at(x), span_y), :], nxt.at[:, x])
        for x in (0, 1, span_x - 2, span_x - 1)
    ]
    both(-3, 0, lambda x: force_plane(s2, field, force, span_y, x))

    table = jnp.concatenate([force[c].astype(BF16) for c in range(3)], axis=1)
    chunk = 256
    upper = lax.broadcasted_iota(jnp.int32, (chunk // 8, 8, depth), 1) < slots
    for i in range(hot.shape[0] // chunk):
        h = hot[pl.ds(i * chunk, chunk), :]
        picked = jnp.dot(h, table, preferred_element_type=F32)
        got = [
            picked[:, c * depth : (c + 1) * depth].reshape(chunk // 8, 8, depth) for c in range(3)
        ]
        both_parts = jnp.concatenate([jnp.where(upper, got[0], got[1]), got[2]], axis=1)
        rows = pl.ds(i * (chunk // 8), chunk // 8)
        sent[rows] = both_parts.astype(BF16)
        one = pltpu.make_async_copy(sent.at[rows], out.at[rows], sent_sems.at[i])
        one.start()
        done.append(one)
    for one in done:
        one.wait()


def flow_kernel(les_x, span_y, flags, vel, wlo, whi, nlo, nhi, base, s0):
    first = 8 * DEEP + 4 * FLAT
    for c in range(3):
        for x in range(les_x):
            s0[c, pl.ds((x + 1) * ROWS + OFF, span_y), :] = vel[c, pl.ds(x * span_y, span_y), :]
        s0[c, pl.ds(OFF, span_y), :] = wlo[first + c] * flags[0]
        s0[c, pl.ds((les_x + 1) * ROWS + OFF, span_y), :] = whi[first + c] * flags[1]
        s0[c, strip(ROWS + OFF - 1, les_x, ROWS), :] = nlo[first + c, pl.ds(0, les_x), :] * flags[2]
        s0[c, strip(ROWS + OFF + span_y, les_x, ROWS), :] = nhi[first + c, pl.ds(0, les_x), :] * flags[3]

    def step(x, carry):
        for t in range(span_y // 8):
            row = (x + 1) * ROWS + OFF + 8 * t
            middle = [s0[c, pl.ds(row, 8), :] for c in range(3)]
            for c in range(3):
                xf = s0[c, pl.ds(row + ROWS, 8), :]
                xb = s0[c, pl.ds(row - ROWS, 8), :]
                yf = s0[c, pl.ds(row + 1, 8), :]
                yb = s0[c, pl.ds(row - 1, 8), :]
                zf, zb = lanes(middle[c])
                carried = 0.5 * (middle[0] * (xf - xb) + middle[1] * (yf - yb) + middle[2] * (zf - zb))
                spread = (xf + xb) + (yf + yb) + (zf + zb) - 6.0 * middle[c]
                base[c, pl.ds(pl.multiple_of(x * span_y + 8 * t, 8), 8), :] = middle[c] + DT * (
                    VISC * spread - carried
                )
        return carry

    lax.fori_loop(0, les_x, step, 0)


def last_kernel(slots, column, got, base, les, nxt):
    lines = base.shape[1]
    depth = got.shape[2]
    wide = got[...].astype(F32)
    values = jnp.concatenate(
        [wide[:, 8 * h : 8 * h + 8, :].reshape(-1, depth).astype(BF16) for h in range(2)], axis=1
    )
    want = column[...]
    lane = lax.broadcasted_iota(jnp.int32, want.shape, 1)
    picked = []
    for half in range(2):
        take = jnp.concatenate(
            [
                jnp.where(want == lane + (depth * k - slots * half), 1.0, 0.0).astype(BF16)
                for k in range(values.shape[0] // depth)
            ],
            axis=1,
        )
        picked.append(jnp.dot(take, values, preferred_element_type=F32))
    for c in range(3):
        push = picked[c % 2][:, (c // 2) * depth : (c // 2 + 1) * depth].astype(BF16)
        les[c] = push
        nxt[c] = base[c] + DT * push.astype(F32)


def call(kernel, out, name, scratch=(), smem=0, count=1, hbm=(), hbm_out=(), alias=None, limit=16):
    vmem = pl.BlockSpec(memory_space=pltpu.VMEM)
    specs = [pl.BlockSpec(memory_space=pltpu.SMEM)] * smem + [vmem] * (count - smem)
    for i in hbm:
        specs[i] = pl.BlockSpec(memory_space=pltpu.HBM)
    return pl.pallas_call(
        kernel,
        out_shape=[jax.ShapeDtypeStruct(shape, kind) for shape, kind in out],
        in_specs=specs,
        out_specs=[
            pl.BlockSpec(memory_space=pltpu.HBM) if i in hbm_out else vmem for i in range(len(out))
        ],
        scratch_shapes=[pltpu.VMEM(*one) if isinstance(one, tuple) else one for one in scratch],
        input_output_aliases=alias or {},
        compiler_params=pltpu.CompilerParams(vmem_limit_bytes=limit * MIB),
        name=name,
    )


def swap(low, high, axis):
    count = lax.axis_size(axis)
    forward = [(i, (i + 1) % count) for i in range(count)]
    backward = [(target, source) for source, target in forward]
    return lax.ppermute(high, axis, forward), lax.ppermute(low, axis, backward)


def body(potential, source_current, cell_label, region_kappa, send_lines, recv_slot, velocity):
    _, span_x, span_y, depth = potential.shape
    les_x = velocity.shape[1]
    peers, slots = send_lines.shape[1:]
    regions = region_kappa.shape[0]
    cells = span_x * span_y
    lines = les_x * span_y
    planes = planes_of()
    vel = velocity.reshape(3, lines, depth)

    wide = ((planes, span_y, depth), F32)
    narrow = ((planes, span_x, depth), F32)
    wlo, whi, nlo, nhi = call(
        functools.partial(faces_kernel, span_x, span_y, regions),
        [wide, wide, narrow, narrow],
        "faces",
        scratch=[
            (potential.shape, F32),
            (source_current.shape, F32),
            (cell_label.shape, jnp.int32),
            (velocity.shape, F32),
            pltpu.SemaphoreType.DMA((4,)),
        ],
        smem=1, count=5, hbm=(1, 2, 3, 4), limit=60,
    )(region_kappa, potential, source_current, cell_label, velocity)
    nlo, nhi = swap(nlo, nhi, "narrow")
    wlo, whi = swap(wlo, whi, "wide")

    corner = ((FLAT * 2 * (8 * DEEP + 4 * FLAT), depth), F32)
    clo, chi = call(
        functools.partial(corner_kernel, span_x), [corner, corner], "corner", count=2
    )(nlo, nhi)
    clo, chi = swap(clo, chi, "wide")

    pad = (span_x + 2 * DEEP) * ROWS + OFF
    padded = ((8, pad, depth), F32)
    fields = ((5, pad, depth), F32)
    w, n = lax.axis_index("wide"), lax.axis_index("narrow")
    flags = jnp.stack(
        [w > 0, w < lax.axis_size("wide") - 1, n > 0, n < lax.axis_size("narrow") - 1]
    ).astype(F32)
    keep = ROWS + OFF
    nxt, halves, nexts, edge_fields, force = call(
        functools.partial(inner_kernel, span_x, span_y, regions),
        [
            (potential.shape, F32),
            ((8, 4 * keep, depth), F32),
            ((8, 4 * keep, depth), F32),
            ((5, 6 * keep, depth), F32),
            ((3, cells, depth), F32),
        ],
        "inner",
        scratch=[
            padded,
            padded,
            padded,
            fields,
            ((3, span_x, span_y, depth), F32),
            ((span_x, span_y, depth), jnp.int32),
            pltpu.SemaphoreType.DMA((2 + 2 * span_x,)),
        ],
        smem=2, count=7, hbm=(2, 3, 4), hbm_out=(0,), limit=LIMIT_IN,
    )(flags, region_kappa, potential, source_current, cell_label, nlo, nhi)

    sent = jnp.concatenate([send_lines[0], send_lines[0]], axis=1).reshape(-1)
    hot = (sent[:, None] == jnp.arange(cells, dtype=jnp.int32)[None, :]).astype(BF16)
    potential_next, outgoing = call(
        functools.partial(outer_kernel, span_x, span_y, slots),
        [(potential.shape, F32), ((peers, 16, depth), BF16)],
        "outer",
        scratch=[
            padded,
            padded,
            padded,
            fields,
            ((3, cells, depth), F32),
            ((peers, 16, depth), BF16),
            pltpu.SemaphoreType.DMA((2 * FLAT + 2 * DEEP + 8,)),
            pltpu.SemaphoreType.DMA((hot.shape[0] // 256,)),
        ],
        smem=1, count=14, hbm=(1, 2, 3, 13), hbm_out=(0, 1), alias={13: 0}, limit=LIMIT_OUT,
    )(flags, potential, wlo, whi, nlo, nhi, clo, chi, hot, halves, nexts, edge_fields, force, nxt)

    incoming = lax.all_to_all(
        outgoing, ("wide", "narrow"), split_axis=0, concat_axis=0, tiled=True
    )
    slot = recv_slot[0]
    column = jnp.broadcast_to(((slot // slots) * 8 + slot % slots)[:, None], (lines, 128))
    (base,) = call(
        functools.partial(flow_kernel, les_x, span_y),
        [((3, lines, depth), F32)],
        "flow",
        scratch=[((3, (les_x + 2) * ROWS + OFF, depth), F32)],
        smem=1, count=6,
    )(flags, vel, wlo, whi, nlo, nhi)
    les, velocity_next = call(
        functools.partial(last_kernel, slots),
        [((3, lines, depth), BF16), ((3, lines, depth), F32)],
        "last", count=3,
    )(column, incoming, base)
    block = (3, les_x, span_y, depth)
    return potential_next, les.reshape(block), velocity_next.reshape(block)


def solution(mesh):
    in_specs = (
        P(None, "wide", "narrow", None),
        P(None, "wide", "narrow", None),
        P("wide", "narrow", None),
        P(),
        P(("wide", "narrow"), None, None),
        P(("wide", "narrow"), None),
        P(None, "wide", "narrow", None),
    )
    out_specs = (
        P(None, "wide", "narrow", None),
        P(None, "wide", "narrow", None),
        P(None, "wide", "narrow", None),
    )
    return jax.shard_map(body, mesh=mesh, in_specs=in_specs, out_specs=out_specs, check_vma=False)
```

```python
import functools

import jax
import jax.numpy as jnp
from jax import lax
from jax.experimental import pallas as pl
from jax.experimental.pallas import tpu as pltpu
from jax.sharding import PartitionSpec as P

DT = 0.25
VISC = 0.5
F32 = jnp.float32
BF16 = jnp.bfloat16
DEEP = 3
FLAT = 2
ROWS = 40
OFF = 8
MIB = 1 << 20
LIMIT_IN = 48
LIMIT_OUT = 48


def strip(start, size, stride):
    return pl.ds(start, size, stride=stride)


def planes_of():
    return 8 * DEEP + 4 * FLAT + 3


def kappa_of(label, rk, regions):
    kappa = jnp.zeros(label.shape, F32)
    for r in range(regions):
        kappa = jnp.where(label == 2 * regions + r, rk[r], kappa)
    return kappa


class Copies:
    def __init__(self, sems):
        self.sems = sems
        self.count = 0

    def start(self, source, target):
        one = pltpu.make_async_copy(source, target, self.sems.at[self.count])
        one.start()
        self.count += 1
        return one


def faces_kernel(
    span_x, span_y, regions, rk, pot, src, lab, vel, wlo, whi, nlo, nhi, all_pot, all_src, all_lab, all_vel, sems
):
    les_x = vel.shape[1]
    flow = 8 * DEEP + 4 * FLAT
    copies = Copies(sems)
    waits = [
        copies.start(source, target)
        for source, target in ((lab, all_lab), (src, all_src), (vel, all_vel), (pot, all_pot))
    ]
    for one in waits[:2]:
        one.wait()
    for side, (wide, narrow) in enumerate(((wlo, nlo), (whi, nhi))):
        for d in range(FLAT):
            x = span_x - FLAT + d if side else d
            y = span_y - 1 - d if side else d
            label = all_lab[x]
            for c in range(3):
                wide[8 * DEEP + 4 * d + c] = jnp.where(label < regions, all_src[c, x], 0.0)
            wide[8 * DEEP + 4 * d + 3] = kappa_of(label, rk, regions)
            label = all_lab[:, y, :]
            for c in range(3):
                narrow[8 * DEEP + 4 * d + c] = jnp.where(label < regions, all_src[c, :, y, :], 0.0)
            narrow[8 * DEEP + 4 * d + 3] = kappa_of(label, rk, regions)
    waits[2].wait()
    for side, (wide, narrow) in enumerate(((wlo, nlo), (whi, nhi))):
        for c in range(3):
            wide[flow + c] = all_vel[c, side * (les_x - 1)]
            narrow[flow + c, pl.ds(0, les_x), :] = all_vel[c, :, side * (span_y - 1), :]
            narrow[flow + c, pl.ds(les_x, span_x - les_x), :] = jnp.zeros((span_x - les_x, vel.shape[3]), F32)
    waits[3].wait()
    for side, (wide, narrow) in enumerate(((wlo, nlo), (whi, nhi))):
        for d in range(DEEP):
            x = span_x - DEEP + d if side else d
            y = span_y - 1 - d if side else d
            for c in range(8):
                wide[8 * d + c] = all_pot[c, x]
                narrow[8 * d + c] = all_pot[c, :, y, :]


def corner_kernel(span_x, nlo, nhi, clo, chi):
    planes = 8 * DEEP + 4 * FLAT
    for d in range(FLAT):
        for side, ref in enumerate((nlo, nhi)):
            rows = pl.ds((d * 2 + side) * planes, planes)
            clo[rows, :] = ref[:planes, d, :]
            chi[rows, :] = ref[:planes, span_x - 1 - d, :]


def place(c, d):
    return 8 * d + c if c < 8 else 8 * DEEP + 4 * d + c - 8


def at(x):
    return (x + DEEP) * ROWS + OFF


def scale_plane(span_x, span_y, flags, field, x):
    line = lax.broadcasted_iota(jnp.int32, (8, field.shape[-1]), 0)
    fx = jnp.where(x < 0, flags[0], jnp.where(x >= span_x, flags[1], 1.0))
    for t in range(5):
        row = at(x) - FLAT + 8 * t
        y = line + (8 * t - FLAT)
        fy = jnp.where(y < 0, flags[2], jnp.where(y >= span_y, flags[3], 1.0))
        kappa = field[3, pl.ds(row, 8), :]
        field[4, pl.ds(row, 8), :] = (fx * fy) / (36.0 + kappa * kappa)


def sweep_plane(old, new, field, x, margin):
    for t in range(5):
        sweep_tile(old, new, field, at(x) - margin + 8 * t)


def over(low, high, do, unroll=1):
    def step(i, carry):
        do(i + low)
        return carry

    lax.fori_loop(0, high - low, step, 0, unroll=unroll)


def lanes(value):
    depth = value.shape[-1]
    lane = lax.broadcasted_iota(jnp.int32, value.shape, 1)
    ahead = jnp.where(lane == depth - 1, 0.0, pltpu.roll(value, depth - 1, 1))
    back = jnp.where(lane == 0, 0.0, pltpu.roll(value, 1, 1))
    return ahead, back


def sweep_tile(old, new, field, row):
    s6 = 6.0 * field[4, pl.ds(row, 8), :]
    kappa = field[3, pl.ds(row, 8), :]
    sk = kappa * field[4, pl.ds(row, 8), :]
    half = 0.5 * kappa
    total = []
    diff = []
    for c in range(8):
        xf = old[c, pl.ds(row + ROWS, 8), :]
        xb = old[c, pl.ds(row - ROWS, 8), :]
        yf = old[c, pl.ds(row + 1, 8), :]
        yb = old[c, pl.ds(row - 1, 8), :]
        zf, zb = lanes(old[c, pl.ds(row, 8), :])
        total.append((xf + xb) + (yf + yb) + (zf + zb))
        if c % 4 == 3:
            diff.append((xf - xb, yf - yb, zf - zb))
        else:
            diff.append(((xf - xb), (yf - yb), (zf - zb))[c % 4])
    for c in range(3):
        first = (field[c, pl.ds(row, 8), :] + total[c]) + half * diff[7][c]
        second = total[4 + c] - half * diff[3][c]
        new[c, pl.ds(row, 8), :] = s6 * first + sk * second
        new[4 + c, pl.ds(row, 8), :] = s6 * second - sk * first
    first = total[3] + half * (diff[4] + diff[5] + diff[6])
    second = total[7] - half * (diff[0] + diff[1] + diff[2])
    new[3, pl.ds(row, 8), :] = s6 * first + sk * second
    new[7, pl.ds(row, 8), :] = s6 * second - sk * first


def lorentz_tile(now, field, row):
    def grab(c, shift):
        return now[c, pl.ds(row + shift, 8), :]

    kappa = field[3, pl.ds(row, 8), :]

    def part(base):
        a = [grab(base + c, 0) for c in range(3)]
        azf, azb = lanes(a[0])
        bzf, bzb = lanes(a[1])
        curl = [
            (grab(base + 2, 1) - grab(base + 2, -1)) - (bzf - bzb),
            (azf - azb) - (grab(base + 2, ROWS) - grab(base + 2, -ROWS)),
            (grab(base + 1, ROWS) - grab(base + 1, -ROWS)) - (grab(base, 1) - grab(base, -1)),
        ]
        phi = grab(base + 3, 0)
        pzf, pzb = lanes(phi)
        grad = [
            grab(base + 3, ROWS) - grab(base + 3, -ROWS),
            grab(base + 3, 1) - grab(base + 3, -1),
            pzf - pzb,
        ]
        return curl, [a[c] + 0.5 * grad[c] for c in range(3)]

    real_b, field_re = part(0)
    imag_b, field_im = part(4)
    cur_re = [field[c, pl.ds(row, 8), :] + kappa * field_im[c] for c in range(3)]
    cur_im = [-kappa * field_re[c] for c in range(3)]
    force = []
    for c in range(3):
        n = (c + 1) % 3
        f = (c + 2) % 3
        value = (cur_re[n] * real_b[f] - cur_re[f] * real_b[n]) + (
            cur_im[n] * imag_b[f] - cur_im[f] * imag_b[n]
        )
        force.append(jnp.where(kappa > 0.0, 0.25 * value, 0.0))
    return force


def force_plane(now, field, force, span_y, x):
    for t in range(span_y // 8):
        f = lorentz_tile(now, field, at(x) + 8 * t)
        rows = pl.ds(pl.multiple_of(x * span_y + 8 * t, 8), 8)
        for c in range(3):
            force[c, rows, :] = f[c]


def stored(x):
    return pl.ds((x + DEEP) * ROWS, ROWS + OFF)


def kept(i):
    return pl.ds(i * (ROWS + OFF), ROWS + OFF)


def inner_kernel(
    span_x, span_y, regions, flags, rk, pot, src, lab, nlo, nhi,
    nxt, halves, nexts, fields, force, s0, s1, s2, field, some, tags, sems,
):
    copies = Copies(sems)
    early = [copies.start(lab, tags), copies.start(src, some)]
    late = [
        copies.start(pot.at[:, x], s0.at[:, pl.ds(at(x), span_y), :]) for x in range(span_x)
    ]
    for c in range(12):
        deep = DEEP if c < 8 else FLAT
        ref, part = (s0, c) if c < 8 else (field, c - 8)
        for d in range(deep):
            ref[part, strip(at(0) - 1 - d, span_x, ROWS), :] = nlo[place(c, d)] * flags[2]
            ref[part, strip(at(0) + span_y + d, span_x, ROWS), :] = nhi[place(c, d)] * flags[3]
    for one in early:
        one.wait()

    def lay(x):
        there = pl.ds(pl.multiple_of((x + DEEP) * ROWS + OFF, 8), span_y)
        label = tags[x]
        for c in range(3):
            field[c, there, :] = jnp.where(label < regions, some[c, x], 0.0)
        field[3, there, :] = kappa_of(label, rk, regions)

    over(0, span_x, lay)
    over(0, span_x, lambda x: scale_plane(span_x, span_y, flags, field, x))
    for one in late:
        one.wait()
    over(1, span_x - 1, lambda x: sweep_plane(s0, s1, field, x, 2), 7)
    over(2, span_x - 2, lambda x: sweep_plane(s1, s2, field, x, 1), 7)
    done = [
        copies.start(s2.at[:, pl.ds(at(x), span_y), :], nxt.at[:, x]) for x in range(2, span_x - 2)
    ]
    over(3, span_x - 3, lambda x: force_plane(s2, field, force, span_y, x), 5)
    for c in range(8):
        for i, x in enumerate((1, 2, span_x - 3, span_x - 2)):
            halves[c, kept(i), :] = s1[c, stored(x), :]
        for i, x in enumerate((2, 3, span_x - 4, span_x - 3)):
            nexts[c, kept(i), :] = s2[c, stored(x), :]
    for c in range(5):
        for i, x in enumerate((0, 1, 2, span_x - 3, span_x - 2, span_x - 1)):
            fields[c, kept(i), :] = field[c, stored(x), :]
    for one in done:
        one.wait()


def outer_kernel(
    span_x, span_y, slots, flags, pot, wlo, whi, nlo, nhi, clo, chi, hot_far, halves, nexts, fields, some_force, old_nxt,
    nxt, out, s0, s1, s2, field, force, sent, hot, sems, sent_sems,
):
    depth = pot.shape[-1]
    planes = 8 * DEEP + 4 * FLAT
    copies = Copies(sems)
    early = []
    late = []
    for d in range(FLAT):
        for ref, x in ((wlo, d - FLAT), (whi, span_x + d)):
            early.append(
                copies.start(ref.at[pl.ds(8 * DEEP + 4 * d, 4)], field.at[pl.ds(0, 4), pl.ds(at(x), span_y), :])
            )
    for d in range(DEEP):
        for ref, x in ((wlo, d - DEEP), (whi, span_x + d)):
            late.append(copies.start(ref.at[pl.ds(8 * d, 8)], s0.at[:, pl.ds(at(x), span_y), :]))
    for x in (0, 1, span_x - 2, span_x - 1):
        late.append(copies.start(pot.at[:, x], s0.at[:, pl.ds(at(x), span_y), :]))
    picks = copies.start(hot_far, hot)
    for c in range(8):
        for i, x in enumerate((1, 2, span_x - 3, span_x - 2)):
            s1[c, stored(x), :] = halves[c, kept(i), :]
        for i, x in enumerate((2, 3, span_x - 4, span_x - 3)):
            s2[c, stored(x), :] = nexts[c, kept(i), :]
    for c in range(3):
        rows = pl.ds(3 * span_y, (span_x - 6) * span_y)
        force[c, rows, :] = some_force[c, rows, :]
    for c in range(8):
        for d in range(DEEP):
            p = place(c, d)
            for x in (0, 1, span_x - 2, span_x - 1):
                s0[c, pl.ds(at(x) - 1 - d, 1), :] = nlo[p, pl.ds(x, 1), :] * flags[2]
                s0[c, pl.ds(at(x) + span_y + d, 1), :] = nhi[p, pl.ds(x, 1), :] * flags[3]
    for one in early:
        one.wait()
    for c in range(5):
        for i, x in enumerate((0, 1, 2, span_x - 3, span_x - 2, span_x - 1)):
            field[c, pl.ds(at(x) - 3, span_y + 6), :] = fields[c, pl.ds(i * (ROWS + OFF) + OFF - 3, span_y + 6), :]
    for c in range(12):
        deep = DEEP if c < 8 else FLAT
        ref, part = (s0, c) if c < 8 else (field, c - 8)
        for d in range(deep - 1):
            for e in range(deep - 1 - d):
                p = place(c, d)
                for source, x in ((clo, -1 - e), (chi, span_x + e)):
                    low, high = (source[pl.ds((e * 2 + side) * planes + p, 1), :] for side in range(2))
                    ref[part, pl.ds(at(x) - 1 - d, 1), :] = low * flags[2]
                    ref[part, pl.ds(at(x) + span_y + d, 1), :] = high * flags[3]

    def both(low, high, do):
        over(-high, -low, do, 3)
        over(span_x + low, span_x + high, do, 3)

    both(0, 2, lambda x: scale_plane(span_x, span_y, flags, field, x))
    for one in late:
        one.wait()
    for i, first in enumerate((-DEEP, span_x)):

        @pl.when(flags[i] == 0.0)
        def _():
            for c in range(8):
                for x in range(first, first + DEEP):
                    s0[c, pl.ds(at(x) - DEEP, span_y + 2 * DEEP), :] = jnp.zeros((span_y + 2 * DEEP, depth), F32)

    both(-1, 2, lambda x: sweep_plane(s0, s1, field, x, 2))
    both(-2, 1, lambda x: sweep_plane(s1, s2, field, x, 1))
    done = [
        copies.start(s2.at[:, pl.ds(at(x), span_y), :], nxt.at[:, x])
        for x in (0, 1, span_x - 2, span_x - 1)
    ]
    both(-3, 0, lambda x: force_plane(s2, field, force, span_y, x))

    picks.wait()
    table = jnp.concatenate([force[c].astype(BF16) for c in range(3)], axis=1)
    chunk = 256
    upper = lax.broadcasted_iota(jnp.int32, (chunk // 8, 8, depth), 1) < slots
    for i in range(hot.shape[0] // chunk):
        h = hot[pl.ds(i * chunk, chunk), :]
        picked = jnp.dot(h, table, preferred_element_type=F32)
        got = [
            picked[:, c * depth : (c + 1) * depth].reshape(chunk // 8, 8, depth) for c in range(3)
        ]
        both_parts = jnp.concatenate([jnp.where(upper, got[0], got[1]), got[2]], axis=1)
        rows = pl.ds(i * (chunk // 8), chunk // 8)
        sent[rows] = both_parts.astype(BF16)
        one = pltpu.make_async_copy(sent.at[rows], out.at[rows], sent_sems.at[i])
        one.start()
        done.append(one)
    for one in done:
        one.wait()


def flow_kernel(les_x, span_y, flags, vel, wlo, whi, nlo, nhi, base, s0):
    first = 8 * DEEP + 4 * FLAT
    for c in range(3):
        for x in range(les_x):
            s0[c, pl.ds((x + 1) * ROWS + OFF, span_y), :] = vel[c, pl.ds(x * span_y, span_y), :]
        s0[c, pl.ds(OFF, span_y), :] = wlo[first + c] * flags[0]
        s0[c, pl.ds((les_x + 1) * ROWS + OFF, span_y), :] = whi[first + c] * flags[1]
        s0[c, strip(ROWS + OFF - 1, les_x, ROWS), :] = nlo[first + c, pl.ds(0, les_x), :] * flags[2]
        s0[c, strip(ROWS + OFF + span_y, les_x, ROWS), :] = nhi[first + c, pl.ds(0, les_x), :] * flags[3]

    def step(x, carry):
        for t in range(span_y // 8):
            row = (x + 1) * ROWS + OFF + 8 * t
            middle = [s0[c, pl.ds(row, 8), :] for c in range(3)]
            for c in range(3):
                xf = s0[c, pl.ds(row + ROWS, 8), :]
                xb = s0[c, pl.ds(row - ROWS, 8), :]
                yf = s0[c, pl.ds(row + 1, 8), :]
                yb = s0[c, pl.ds(row - 1, 8), :]
                zf, zb = lanes(middle[c])
                carried = 0.5 * (middle[0] * (xf - xb) + middle[1] * (yf - yb) + middle[2] * (zf - zb))
                spread = (xf + xb) + (yf + yb) + (zf + zb) - 6.0 * middle[c]
                base[c, pl.ds(pl.multiple_of(x * span_y + 8 * t, 8), 8), :] = middle[c] + DT * (
                    VISC * spread - carried
                )
        return carry

    lax.fori_loop(0, les_x, step, 0)


def last_kernel(slots, column, got, base, les, nxt):
    lines = base.shape[1]
    depth = got.shape[2]
    wide = got[...].astype(F32)
    values = jnp.concatenate(
        [wide[:, 8 * h : 8 * h + 8, :].reshape(-1, depth).astype(BF16) for h in range(2)], axis=1
    )
    want = column[...]
    lane = lax.broadcasted_iota(jnp.int32, want.shape, 1)
    picked = []
    for half in range(2):
        take = jnp.concatenate(
            [
                jnp.where(want == lane + (depth * k - slots * half), 1.0, 0.0).astype(BF16)
                for k in range(values.shape[0] // depth)
            ],
            axis=1,
        )
        picked.append(jnp.dot(take, values, preferred_element_type=F32))
    for c in range(3):
        push = picked[c % 2][:, (c // 2) * depth : (c // 2 + 1) * depth].astype(BF16)
        les[c] = push
        nxt[c] = base[c] + DT * push.astype(F32)


def call(kernel, out, name, scratch=(), smem=0, count=1, hbm=(), hbm_out=(), alias=None, limit=16):
    vmem = pl.BlockSpec(memory_space=pltpu.VMEM)
    specs = [pl.BlockSpec(memory_space=pltpu.SMEM)] * smem + [vmem] * (count - smem)
    for i in hbm:
        specs[i] = pl.BlockSpec(memory_space=pltpu.HBM)
    return pl.pallas_call(
        kernel,
        out_shape=[jax.ShapeDtypeStruct(shape, kind) for shape, kind in out],
        in_specs=specs,
        out_specs=[
            pl.BlockSpec(memory_space=pltpu.HBM) if i in hbm_out else vmem for i in range(len(out))
        ],
        scratch_shapes=[pltpu.VMEM(*one) if isinstance(one, tuple) else one for one in scratch],
        input_output_aliases=alias or {},
        compiler_params=pltpu.CompilerParams(vmem_limit_bytes=limit * MIB),
        name=name,
    )


def swap(low, high, axis):
    count = lax.axis_size(axis)
    forward = [(i, (i + 1) % count) for i in range(count)]
    backward = [(target, source) for source, target in forward]
    return lax.ppermute(high, axis, forward), lax.ppermute(low, axis, backward)


def body(potential, source_current, cell_label, region_kappa, send_lines, recv_slot, velocity):
    _, span_x, span_y, depth = potential.shape
    les_x = velocity.shape[1]
    peers, slots = send_lines.shape[1:]
    regions = region_kappa.shape[0]
    cells = span_x * span_y
    lines = les_x * span_y
    planes = planes_of()
    vel = velocity.reshape(3, lines, depth)

    wide = ((planes, span_y, depth), F32)
    narrow = ((planes, span_x, depth), F32)
    wlo, whi, nlo, nhi = call(
        functools.partial(faces_kernel, span_x, span_y, regions),
        [wide, wide, narrow, narrow],
        "faces",
        scratch=[
            (potential.shape, F32),
            (source_current.shape, F32),
            (cell_label.shape, jnp.int32),
            (velocity.shape, F32),
            pltpu.SemaphoreType.DMA((4,)),
        ],
        smem=1, count=5, hbm=(1, 2, 3, 4), limit=60,
    )(region_kappa, potential, source_current, cell_label, velocity)
    nlo, nhi = swap(nlo, nhi, "narrow")
    wlo, whi = swap(wlo, whi, "wide")

    corner = ((FLAT * 2 * (8 * DEEP + 4 * FLAT), depth), F32)
    clo, chi = call(
        functools.partial(corner_kernel, span_x), [corner, corner], "corner", count=2
    )(nlo, nhi)
    clo, chi = swap(clo, chi, "wide")

    pad = (span_x + 2 * DEEP) * ROWS + OFF
    padded = ((8, pad, depth), F32)
    fields = ((5, pad, depth), F32)
    w, n = lax.axis_index("wide"), lax.axis_index("narrow")
    flags = jnp.stack(
        [w > 0, w < lax.axis_size("wide") - 1, n > 0, n < lax.axis_size("narrow") - 1]
    ).astype(F32)
    keep = ROWS + OFF
    nxt, halves, nexts, edge_fields, force = call(
        functools.partial(inner_kernel, span_x, span_y, regions),
        [
            (potential.shape, F32),
            ((8, 4 * keep, depth), F32),
            ((8, 4 * keep, depth), F32),
            ((5, 6 * keep, depth), F32),
            ((3, cells, depth), F32),
        ],
        "inner",
        scratch=[
            padded,
            padded,
            padded,
            fields,
            ((3, span_x, span_y, depth), F32),
            ((span_x, span_y, depth), jnp.int32),
            pltpu.SemaphoreType.DMA((2 + 2 * span_x,)),
        ],
        smem=2, count=7, hbm=(2, 3, 4), hbm_out=(0,), limit=LIMIT_IN,
    )(flags, region_kappa, potential, source_current, cell_label, nlo, nhi)

    sent = jnp.concatenate([send_lines[0], send_lines[0]], axis=1).reshape(-1)
    hot = (sent[:, None] == jnp.arange(cells, dtype=jnp.int32)[None, :]).astype(BF16)
    potential_next, outgoing = call(
        functools.partial(outer_kernel, span_x, span_y, slots),
        [(potential.shape, F32), ((peers, 16, depth), BF16)],
        "outer",
        scratch=[
            padded,
            padded,
            padded,
            fields,
            ((3, cells, depth), F32),
            ((peers, 16, depth), BF16),
            (hot.shape, BF16),
            pltpu.SemaphoreType.DMA((2 * FLAT + 2 * DEEP + 9,)),
            pltpu.SemaphoreType.DMA((hot.shape[0] // 256,)),
        ],
        smem=1, count=14, hbm=(1, 2, 3, 8, 13), hbm_out=(0, 1), alias={13: 0}, limit=LIMIT_OUT,
    )(flags, potential, wlo, whi, nlo, nhi, clo, chi, hot, halves, nexts, edge_fields, force, nxt)

    incoming = lax.all_to_all(
        outgoing, ("wide", "narrow"), split_axis=0, concat_axis=0, tiled=True
    )
    slot = recv_slot[0]
    column = jnp.broadcast_to(((slot // slots) * 8 + slot % slots)[:, None], (lines, 128))
    (base,) = call(
        functools.partial(flow_kernel, les_x, span_y),
        [((3, lines, depth), F32)],
        "flow",
        scratch=[((3, (les_x + 2) * ROWS + OFF, depth), F32)],
        smem=1, count=6,
    )(flags, vel, wlo, whi, nlo, nhi)
    les, velocity_next = call(
        functools.partial(last_kernel, slots),
        [((3, lines, depth), BF16), ((3, lines, depth), F32)],
        "last", count=3,
    )(column, incoming, base)
    block = (3, les_x, span_y, depth)
    return potential_next, les.reshape(block), velocity_next.reshape(block)


def solution(mesh):
    in_specs = (
        P(None, "wide", "narrow", None),
        P(None, "wide", "narrow", None),
        P("wide", "narrow", None),
        P(),
        P(("wide", "narrow"), None, None),
        P(("wide", "narrow"), None),
        P(None, "wide", "narrow", None),
    )
    out_specs = (
        P(None, "wide", "narrow", None),
        P(None, "wide", "narrow", None),
        P(None, "wide", "narrow", None),
    )
    return jax.shard_map(body, mesh=mesh, in_specs=in_specs, out_specs=out_specs, check_vma=False)
```

```python
import functools

import jax
import jax.numpy as jnp
from jax import lax
from jax.experimental import pallas as pl
from jax.experimental.pallas import tpu as pltpu
from jax.sharding import PartitionSpec as P

DT = 0.25
VISC = 0.5
F32 = jnp.float32
BF16 = jnp.bfloat16
DEEP = 3
FLAT = 2
ROWS = 40
OFF = 8
MIB = 1 << 20
LIMIT_IN = 48
LIMIT_OUT = 48


def strip(start, size, stride):
    return pl.ds(start, size, stride=stride)


def planes_of():
    return 8 * DEEP + 4 * FLAT + 3


def kappa_of(label, rk, regions):
    kappa = jnp.zeros(label.shape, F32)
    for r in range(regions):
        kappa = jnp.where(label == 2 * regions + r, rk[r], kappa)
    return kappa


class Copies:
    def __init__(self, sems):
        self.sems = sems
        self.count = 0

    def start(self, source, target):
        one = pltpu.make_async_copy(source, target, self.sems.at[self.count])
        one.start()
        self.count += 1
        return one


def faces_kernel(
    span_x, span_y, regions, rk, pot, src, lab, vel, wlo, whi, nlo, nhi, all_pot, all_src, all_lab, all_vel, sems
):
    les_x = vel.shape[1]
    flow = 8 * DEEP + 4 * FLAT
    copies = Copies(sems)
    waits = [
        copies.start(source, target)
        for source, target in ((lab, all_lab), (src, all_src), (vel, all_vel), (pot, all_pot))
    ]
    for one in waits[:2]:
        one.wait()
    for side, (wide, narrow) in enumerate(((wlo, nlo), (whi, nhi))):
        for d in range(FLAT):
            x = span_x - FLAT + d if side else d
            y = span_y - 1 - d if side else d
            label = all_lab[x]
            for c in range(3):
                wide[8 * DEEP + 4 * d + c] = jnp.where(label < regions, all_src[c, x], 0.0)
            wide[8 * DEEP + 4 * d + 3] = kappa_of(label, rk, regions)
            label = all_lab[:, y, :]
            for c in range(3):
                narrow[8 * DEEP + 4 * d + c] = jnp.where(label < regions, all_src[c, :, y, :], 0.0)
            narrow[8 * DEEP + 4 * d + 3] = kappa_of(label, rk, regions)
    waits[2].wait()
    for side, (wide, narrow) in enumerate(((wlo, nlo), (whi, nhi))):
        for c in range(3):
            wide[flow + c] = all_vel[c, side * (les_x - 1)]
            narrow[flow + c, pl.ds(0, les_x), :] = all_vel[c, :, side * (span_y - 1), :]
            narrow[flow + c, pl.ds(les_x, span_x - les_x), :] = jnp.zeros((span_x - les_x, vel.shape[3]), F32)
    waits[3].wait()
    for side, (wide, narrow) in enumerate(((wlo, nlo), (whi, nhi))):
        for d in range(DEEP):
            x = span_x - DEEP + d if side else d
            y = span_y - 1 - d if side else d
            for c in range(8):
                wide[8 * d + c] = all_pot[c, x]
                narrow[8 * d + c] = all_pot[c, :, y, :]


def corner_kernel(span_x, nlo, nhi, clo, chi):
    flat = 8 * DEEP
    for side, ref in enumerate((nlo, nhi)):
        for out, x, beyond in ((clo, 0, 1), (chi, span_x - 1, span_x - 2)):
            out[pl.ds(32 * side, 16), :] = ref[:16, x, :]
            out[pl.ds(32 * side + 16, 8), :] = ref[:8, beyond, :]
            out[pl.ds(32 * side + 24, 8), :] = ref[flat : flat + 8, x, :]


def corner_row(side, c, d, e):
    return 32 * side + (24 + c - 8 if c >= 8 else 8 * d + c if e == 0 else 16 + c)


def place(c, d):
    return 8 * d + c if c < 8 else 8 * DEEP + 4 * d + c - 8


def at(x):
    return (x + DEEP) * ROWS + OFF


def scale_plane(span_x, span_y, flags, field, x):
    line = lax.broadcasted_iota(jnp.int32, (8, field.shape[-1]), 0)
    fx = jnp.where(x < 0, flags[0], jnp.where(x >= span_x, flags[1], 1.0))
    for t in range(5):
        row = at(x) - FLAT + 8 * t
        y = line + (8 * t - FLAT)
        fy = jnp.where(y < 0, flags[2], jnp.where(y >= span_y, flags[3], 1.0))
        kappa = field[3, pl.ds(row, 8), :]
        field[4, pl.ds(row, 8), :] = (fx * fy) / (36.0 + kappa * kappa)


def sweep_plane(old, new, field, x, margin):
    for t in range(5):
        sweep_tile(old, new, field, at(x) - margin + 8 * t)


def over(low, high, do, unroll=1):
    def step(i, carry):
        do(i + low)
        return carry

    lax.fori_loop(0, high - low, step, 0, unroll=unroll)


def lanes(value):
    depth = value.shape[-1]
    lane = lax.broadcasted_iota(jnp.int32, value.shape, 1)
    ahead = jnp.where(lane == depth - 1, 0.0, pltpu.roll(value, depth - 1, 1))
    back = jnp.where(lane == 0, 0.0, pltpu.roll(value, 1, 1))
    return ahead, back


def sweep_tile(old, new, field, row):
    s6 = 6.0 * field[4, pl.ds(row, 8), :]
    kappa = field[3, pl.ds(row, 8), :]
    sk = kappa * field[4, pl.ds(row, 8), :]
    half = 0.5 * kappa
    total = []
    diff = []
    for c in range(8):
        xf = old[c, pl.ds(row + ROWS, 8), :]
        xb = old[c, pl.ds(row - ROWS, 8), :]
        yf = old[c, pl.ds(row + 1, 8), :]
        yb = old[c, pl.ds(row - 1, 8), :]
        zf, zb = lanes(old[c, pl.ds(row, 8), :])
        total.append((xf + xb) + (yf + yb) + (zf + zb))
        if c % 4 == 3:
            diff.append((xf - xb, yf - yb, zf - zb))
        else:
            diff.append(((xf - xb), (yf - yb), (zf - zb))[c % 4])
    for c in range(3):
        first = (field[c, pl.ds(row, 8), :] + total[c]) + half * diff[7][c]
        second = total[4 + c] - half * diff[3][c]
        new[c, pl.ds(row, 8), :] = s6 * first + sk * second
        new[4 + c, pl.ds(row, 8), :] = s6 * second - sk * first
    first = total[3] + half * (diff[4] + diff[5] + diff[6])
    second = total[7] - half * (diff[0] + diff[1] + diff[2])
    new[3, pl.ds(row, 8), :] = s6 * first + sk * second
    new[7, pl.ds(row, 8), :] = s6 * second - sk * first


def lorentz_tile(now, field, row):
    def grab(c, shift):
        return now[c, pl.ds(row + shift, 8), :]

    kappa = field[3, pl.ds(row, 8), :]

    def part(base):
        a = [grab(base + c, 0) for c in range(3)]
        azf, azb = lanes(a[0])
        bzf, bzb = lanes(a[1])
        curl = [
            (grab(base + 2, 1) - grab(base + 2, -1)) - (bzf - bzb),
            (azf - azb) - (grab(base + 2, ROWS) - grab(base + 2, -ROWS)),
            (grab(base + 1, ROWS) - grab(base + 1, -ROWS)) - (grab(base, 1) - grab(base, -1)),
        ]
        phi = grab(base + 3, 0)
        pzf, pzb = lanes(phi)
        grad = [
            grab(base + 3, ROWS) - grab(base + 3, -ROWS),
            grab(base + 3, 1) - grab(base + 3, -1),
            pzf - pzb,
        ]
        return curl, [a[c] + 0.5 * grad[c] for c in range(3)]

    real_b, field_re = part(0)
    imag_b, field_im = part(4)
    cur_re = [field[c, pl.ds(row, 8), :] + kappa * field_im[c] for c in range(3)]
    cur_im = [-kappa * field_re[c] for c in range(3)]
    force = []
    for c in range(3):
        n = (c + 1) % 3
        f = (c + 2) % 3
        value = (cur_re[n] * real_b[f] - cur_re[f] * real_b[n]) + (
            cur_im[n] * imag_b[f] - cur_im[f] * imag_b[n]
        )
        force.append(jnp.where(kappa > 0.0, 0.25 * value, 0.0))
    return force


def force_plane(now, field, force, span_y, x):
    for t in range(span_y // 8):
        f = lorentz_tile(now, field, at(x) + 8 * t)
        rows = pl.ds(pl.multiple_of(x * span_y + 8 * t, 8), 8)
        for c in range(3):
            force[c, rows, :] = f[c]


def stored(x):
    return pl.ds((x + DEEP) * ROWS, ROWS + OFF)


def kept(i):
    return pl.ds(i * (ROWS + OFF), ROWS + OFF)


def inner_kernel(
    span_x, span_y, regions, flags, rk, pot, src, lab, nlo, nhi,
    nxt, halves, nexts, fields, force, s0, s1, s2, field, some, tags, sems,
):
    copies = Copies(sems)
    early = [copies.start(lab, tags), copies.start(src, some)]
    late = [
        copies.start(pot.at[:, x], s0.at[:, pl.ds(at(x), span_y), :]) for x in range(span_x)
    ]
    for c in range(12):
        deep = DEEP if c < 8 else FLAT
        ref, part = (s0, c) if c < 8 else (field, c - 8)
        for d in range(deep):
            ref[part, strip(at(0) - 1 - d, span_x, ROWS), :] = nlo[place(c, d)] * flags[2]
            ref[part, strip(at(0) + span_y + d, span_x, ROWS), :] = nhi[place(c, d)] * flags[3]
    for one in early:
        one.wait()

    def lay(x):
        there = pl.ds(pl.multiple_of((x + DEEP) * ROWS + OFF, 8), span_y)
        label = tags[x]
        for c in range(3):
            field[c, there, :] = jnp.where(label < regions, some[c, x], 0.0)
        field[3, there, :] = kappa_of(label, rk, regions)

    over(0, span_x, lay)
    over(0, span_x, lambda x: scale_plane(span_x, span_y, flags, field, x))
    for one in late:
        one.wait()
    over(1, span_x - 1, lambda x: sweep_plane(s0, s1, field, x, 2), 7)
    over(2, span_x - 2, lambda x: sweep_plane(s1, s2, field, x, 1), 7)
    done = [
        copies.start(s2.at[:, pl.ds(at(x), span_y), :], nxt.at[:, x]) for x in range(2, span_x - 2)
    ]
    over(3, span_x - 3, lambda x: force_plane(s2, field, force, span_y, x), 5)
    for c in range(8):
        for i, x in enumerate((1, 2, span_x - 3, span_x - 2)):
            halves[c, kept(i), :] = s1[c, stored(x), :]
        for i, x in enumerate((2, 3, span_x - 4, span_x - 3)):
            nexts[c, kept(i), :] = s2[c, stored(x), :]
    for c in range(5):
        for i, x in enumerate((0, 1, 2, span_x - 3, span_x - 2, span_x - 1)):
            fields[c, kept(i), :] = field[c, stored(x), :]
    for one in done:
        one.wait()


def outer_kernel(
    span_x, span_y, slots, flags, pot, wlo, whi, nlo, nhi, clo, chi, hot_far, halves, nexts, fields, some_force, old_nxt,
    nxt, out, s0, s1, s2, field, force, sent, hot, sems, sent_sems,
):
    depth = pot.shape[-1]
    planes = 8 * DEEP + 4 * FLAT
    copies = Copies(sems)
    early = []
    late = []
    for d in range(FLAT):
        for ref, x in ((wlo, d - FLAT), (whi, span_x + d)):
            early.append(
                copies.start(ref.at[pl.ds(8 * DEEP + 4 * d, 4)], field.at[pl.ds(0, 4), pl.ds(at(x), span_y), :])
            )
    for d in range(DEEP):
        for ref, x in ((wlo, d - DEEP), (whi, span_x + d)):
            late.append(copies.start(ref.at[pl.ds(8 * d, 8)], s0.at[:, pl.ds(at(x), span_y), :]))
    for x in (0, 1, span_x - 2, span_x - 1):
        late.append(copies.start(pot.at[:, x], s0.at[:, pl.ds(at(x), span_y), :]))
    picks = copies.start(hot_far, hot)
    for c in range(8):
        for i, x in enumerate((1, 2, span_x - 3, span_x - 2)):
            s1[c, stored(x), :] = halves[c, kept(i), :]
        for i, x in enumerate((2, 3, span_x - 4, span_x - 3)):
            s2[c, stored(x), :] = nexts[c, kept(i), :]
    for c in range(3):
        rows = pl.ds(3 * span_y, (span_x - 6) * span_y)
        force[c, rows, :] = some_force[c, rows, :]
    for c in range(8):
        for d in range(DEEP):
            p = place(c, d)
            for x in (0, 1, span_x - 2, span_x - 1):
                s0[c, pl.ds(at(x) - 1 - d, 1), :] = nlo[p, pl.ds(x, 1), :] * flags[2]
                s0[c, pl.ds(at(x) + span_y + d, 1), :] = nhi[p, pl.ds(x, 1), :] * flags[3]
    for one in early:
        one.wait()
    for c in range(5):
        for i, x in enumerate((0, 1, 2, span_x - 3, span_x - 2, span_x - 1)):
            field[c, pl.ds(at(x) - 3, span_y + 6), :] = fields[c, pl.ds(i * (ROWS + OFF) + OFF - 3, span_y + 6), :]
    for c in range(12):
        deep = DEEP if c < 8 else FLAT
        ref, part = (s0, c) if c < 8 else (field, c - 8)
        for d in range(deep - 1):
            for e in range(deep - 1 - d):
                p = place(c, d)
                for source, x in ((clo, -1 - e), (chi, span_x + e)):
                    low, high = (source[pl.ds(corner_row(side, c, d, e), 1), :] for side in range(2))
                    ref[part, pl.ds(at(x) - 1 - d, 1), :] = low * flags[2]
                    ref[part, pl.ds(at(x) + span_y + d, 1), :] = high * flags[3]

    def both(low, high, do):
        over(-high, -low, do, 3)
        over(span_x + low, span_x + high, do, 3)

    both(0, 2, lambda x: scale_plane(span_x, span_y, flags, field, x))
    for one in late:
        one.wait()
    for i, first in enumerate((-DEEP, span_x)):

        @pl.when(flags[i] == 0.0)
        def _():
            for c in range(8):
                for x in range(first, first + DEEP):
                    s0[c, pl.ds(at(x) - DEEP, span_y + 2 * DEEP), :] = jnp.zeros((span_y + 2 * DEEP, depth), F32)

    both(-1, 2, lambda x: sweep_plane(s0, s1, field, x, 2))
    both(-2, 1, lambda x: sweep_plane(s1, s2, field, x, 1))
    done = [
        copies.start(s2.at[:, pl.ds(at(x), span_y), :], nxt.at[:, x])
        for x in (0, 1, span_x - 2, span_x - 1)
    ]
    both(-3, 0, lambda x: force_plane(s2, field, force, span_y, x))

    picks.wait()
    table = jnp.concatenate([force[c].astype(BF16) for c in range(3)], axis=1)
    chunk = 256
    upper = lax.broadcasted_iota(jnp.int32, (chunk // 8, 8, depth), 1) < slots
    for i in range(hot.shape[0] // chunk):
        h = hot[pl.ds(i * chunk, chunk), :]
        picked = jnp.dot(h, table, preferred_element_type=F32)
        got = [
            picked[:, c * depth : (c + 1) * depth].reshape(chunk // 8, 8, depth) for c in range(3)
        ]
        both_parts = jnp.concatenate([jnp.where(upper, got[0], got[1]), got[2]], axis=1)
        rows = pl.ds(i * (chunk // 8), chunk // 8)
        sent[rows] = both_parts.astype(BF16)
        one = pltpu.make_async_copy(sent.at[rows], out.at[rows], sent_sems.at[i])
        one.start()
        done.append(one)
    for one in done:
        one.wait()


def flow_kernel(les_x, span_y, flags, vel, wlo, whi, nlo, nhi, base, s0):
    first = 8 * DEEP + 4 * FLAT
    for c in range(3):
        for x in range(les_x):
            s0[c, pl.ds((x + 1) * ROWS + OFF, span_y), :] = vel[c, pl.ds(x * span_y, span_y), :]
        s0[c, pl.ds(OFF, span_y), :] = wlo[first + c] * flags[0]
        s0[c, pl.ds((les_x + 1) * ROWS + OFF, span_y), :] = whi[first + c] * flags[1]
        s0[c, strip(ROWS + OFF - 1, les_x, ROWS), :] = nlo[first + c, pl.ds(0, les_x), :] * flags[2]
        s0[c, strip(ROWS + OFF + span_y, les_x, ROWS), :] = nhi[first + c, pl.ds(0, les_x), :] * flags[3]

    def step(x, carry):
        for t in range(span_y // 8):
            row = (x + 1) * ROWS + OFF + 8 * t
            middle = [s0[c, pl.ds(row, 8), :] for c in range(3)]
            for c in range(3):
                xf = s0[c, pl.ds(row + ROWS, 8), :]
                xb = s0[c, pl.ds(row - ROWS, 8), :]
                yf = s0[c, pl.ds(row + 1, 8), :]
                yb = s0[c, pl.ds(row - 1, 8), :]
                zf, zb = lanes(middle[c])
                carried = 0.5 * (middle[0] * (xf - xb) + middle[1] * (yf - yb) + middle[2] * (zf - zb))
                spread = (xf + xb) + (yf + yb) + (zf + zb) - 6.0 * middle[c]
                base[c, pl.ds(pl.multiple_of(x * span_y + 8 * t, 8), 8), :] = middle[c] + DT * (
                    VISC * spread - carried
                )
        return carry

    lax.fori_loop(0, les_x, step, 0)


def last_kernel(slots, column, got, base, les, nxt):
    lines = base.shape[1]
    depth = got.shape[2]
    wide = got[...].astype(F32)
    values = jnp.concatenate(
        [wide[:, 8 * h : 8 * h + 8, :].reshape(-1, depth).astype(BF16) for h in range(2)], axis=1
    )
    want = column[...]
    lane = lax.broadcasted_iota(jnp.int32, want.shape, 1)
    picked = []
    for half in range(2):
        take = jnp.concatenate(
            [
                jnp.where(want == lane + (depth * k - slots * half), 1.0, 0.0).astype(BF16)
                for k in range(values.shape[0] // depth)
            ],
            axis=1,
        )
        picked.append(jnp.dot(take, values, preferred_element_type=F32))
    for c in range(3):
        push = picked[c % 2][:, (c // 2) * depth : (c // 2 + 1) * depth].astype(BF16)
        les[c] = push
        nxt[c] = base[c] + DT * push.astype(F32)


def call(kernel, out, name, scratch=(), smem=0, count=1, hbm=(), hbm_out=(), alias=None, limit=16):
    vmem = pl.BlockSpec(memory_space=pltpu.VMEM)
    specs = [pl.BlockSpec(memory_space=pltpu.SMEM)] * smem + [vmem] * (count - smem)
    for i in hbm:
        specs[i] = pl.BlockSpec(memory_space=pltpu.HBM)
    return pl.pallas_call(
        kernel,
        out_shape=[jax.ShapeDtypeStruct(shape, kind) for shape, kind in out],
        in_specs=specs,
        out_specs=[
            pl.BlockSpec(memory_space=pltpu.HBM) if i in hbm_out else vmem for i in range(len(out))
        ],
        scratch_shapes=[pltpu.VMEM(*one) if isinstance(one, tuple) else one for one in scratch],
        input_output_aliases=alias or {},
        compiler_params=pltpu.CompilerParams(vmem_limit_bytes=limit * MIB),
        name=name,
    )


def swap(low, high, axis):
    count = lax.axis_size(axis)
    forward = [(i, (i + 1) % count) for i in range(count)]
    backward = [(target, source) for source, target in forward]
    return lax.ppermute(high, axis, forward), lax.ppermute(low, axis, backward)


def body(potential, source_current, cell_label, region_kappa, send_lines, recv_slot, velocity):
    _, span_x, span_y, depth = potential.shape
    les_x = velocity.shape[1]
    peers, slots = send_lines.shape[1:]
    regions = region_kappa.shape[0]
    cells = span_x * span_y
    lines = les_x * span_y
    planes = planes_of()
    vel = velocity.reshape(3, lines, depth)

    wide = ((planes, span_y, depth), F32)
    narrow = ((planes, span_x, depth), F32)
    wlo, whi, nlo, nhi = call(
        functools.partial(faces_kernel, span_x, span_y, regions),
        [wide, wide, narrow, narrow],
        "faces",
        scratch=[
            (potential.shape, F32),
            (source_current.shape, F32),
            (cell_label.shape, jnp.int32),
            (velocity.shape, F32),
            pltpu.SemaphoreType.DMA((4,)),
        ],
        smem=1, count=5, hbm=(1, 2, 3, 4), limit=60,
    )(region_kappa, potential, source_current, cell_label, velocity)
    nlo, nhi = swap(nlo, nhi, "narrow")
    wlo, whi = swap(wlo, whi, "wide")

    corner = ((64, depth), F32)
    clo, chi = call(
        functools.partial(corner_kernel, span_x), [corner, corner], "corner", count=2
    )(nlo, nhi)
    clo, chi = swap(clo, chi, "wide")

    pad = (span_x + 2 * DEEP) * ROWS + OFF
    padded = ((8, pad, depth), F32)
    fields = ((5, pad, depth), F32)
    w, n = lax.axis_index("wide"), lax.axis_index("narrow")
    flags = jnp.stack(
        [w > 0, w < lax.axis_size("wide") - 1, n > 0, n < lax.axis_size("narrow") - 1]
    ).astype(F32)
    keep = ROWS + OFF
    nxt, halves, nexts, edge_fields, force = call(
        functools.partial(inner_kernel, span_x, span_y, regions),
        [
            (potential.shape, F32),
            ((8, 4 * keep, depth), F32),
            ((8, 4 * keep, depth), F32),
            ((5, 6 * keep, depth), F32),
            ((3, cells, depth), F32),
        ],
        "inner",
        scratch=[
            padded,
            padded,
            padded,
            fields,
            ((3, span_x, span_y, depth), F32),
            ((span_x, span_y, depth), jnp.int32),
            pltpu.SemaphoreType.DMA((2 + 2 * span_x,)),
        ],
        smem=2, count=7, hbm=(2, 3, 4), hbm_out=(0,), limit=LIMIT_IN,
    )(flags, region_kappa, potential, source_current, cell_label, nlo, nhi)

    sent = jnp.concatenate([send_lines[0], send_lines[0]], axis=1).reshape(-1)
    hot = (sent[:, None] == jnp.arange(cells, dtype=jnp.int32)[None, :]).astype(BF16)
    potential_next, outgoing = call(
        functools.partial(outer_kernel, span_x, span_y, slots),
        [(potential.shape, F32), ((peers, 16, depth), BF16)],
        "outer",
        scratch=[
            padded,
            padded,
            padded,
            fields,
            ((3, cells, depth), F32),
            ((peers, 16, depth), BF16),
            (hot.shape, BF16),
            pltpu.SemaphoreType.DMA((2 * FLAT + 2 * DEEP + 9,)),
            pltpu.SemaphoreType.DMA((hot.shape[0] // 256,)),
        ],
        smem=1, count=14, hbm=(1, 2, 3, 8, 13), hbm_out=(0, 1), alias={13: 0}, limit=LIMIT_OUT,
    )(flags, potential, wlo, whi, nlo, nhi, clo, chi, hot, halves, nexts, edge_fields, force, nxt)

    incoming = lax.all_to_all(
        outgoing, ("wide", "narrow"), split_axis=0, concat_axis=0, tiled=True
    )
    slot = recv_slot[0]
    column = jnp.broadcast_to(((slot // slots) * 8 + slot % slots)[:, None], (lines, 128))
    (base,) = call(
        functools.partial(flow_kernel, les_x, span_y),
        [((3, lines, depth), F32)],
        "flow",
        scratch=[((3, (les_x + 2) * ROWS + OFF, depth), F32)],
        smem=1, count=6,
    )(flags, vel, wlo, whi, nlo, nhi)
    les, velocity_next = call(
        functools.partial(last_kernel, slots),
        [((3, lines, depth), BF16), ((3, lines, depth), F32)],
        "last", count=3,
    )(column, incoming, base)
    block = (3, les_x, span_y, depth)
    return potential_next, les.reshape(block), velocity_next.reshape(block)


def solution(mesh):
    in_specs = (
        P(None, "wide", "narrow", None),
        P(None, "wide", "narrow", None),
        P("wide", "narrow", None),
        P(),
        P(("wide", "narrow"), None, None),
        P(("wide", "narrow"), None),
        P(None, "wide", "narrow", None),
    )
    out_specs = (
        P(None, "wide", "narrow", None),
        P(None, "wide", "narrow", None),
        P(None, "wide", "narrow", None),
    )
    return jax.shard_map(body, mesh=mesh, in_specs=in_specs, out_specs=out_specs, check_vma=False)
```

```python
import functools

import jax
import jax.numpy as jnp
from jax import lax
from jax.experimental import pallas as pl
from jax.experimental.pallas import tpu as pltpu
from jax.sharding import PartitionSpec as P

DT = 0.25
VISC = 0.5
F32 = jnp.float32
BF16 = jnp.bfloat16
DEEP = 3
FLAT = 2
ROWS = 40
OFF = 8
MIB = 1 << 20
LIMIT_IN = 48
LIMIT_OUT = 48


def strip(start, size, stride):
    return pl.ds(start, size, stride=stride)


def planes_of():
    return 8 * DEEP + 4 * FLAT + 3


def kappa_of(label, rk, regions):
    kappa = jnp.zeros(label.shape, F32)
    for r in range(regions):
        kappa = jnp.where(label == 2 * regions + r, rk[r], kappa)
    return kappa


class Copies:
    def __init__(self, sems):
        self.sems = sems
        self.count = 0

    def start(self, source, target):
        one = pltpu.make_async_copy(source, target, self.sems.at[self.count])
        one.start()
        self.count += 1
        return one


def faces_kernel(
    span_x, span_y, regions, rk, pot, src, lab, vel, wlo, whi, nlo, nhi, all_pot, all_src, all_lab, all_vel, sems
):
    les_x = vel.shape[1]
    flow = 8 * DEEP + 4 * FLAT
    copies = Copies(sems)
    waits = [
        copies.start(source, target)
        for source, target in ((lab, all_lab), (src, all_src), (vel, all_vel), (pot, all_pot))
    ]
    for one in waits[:2]:
        one.wait()
    for side, (wide, narrow) in enumerate(((wlo, nlo), (whi, nhi))):
        for d in range(FLAT):
            x = span_x - FLAT + d if side else d
            y = span_y - 1 - d if side else d
            label = all_lab[x]
            for c in range(3):
                wide[8 * DEEP + 4 * d + c] = jnp.where(label < regions, all_src[c, x], 0.0)
            wide[8 * DEEP + 4 * d + 3] = kappa_of(label, rk, regions)
            label = all_lab[:, y, :]
            for c in range(3):
                narrow[8 * DEEP + 4 * d + c] = jnp.where(label < regions, all_src[c, :, y, :], 0.0)
            narrow[8 * DEEP + 4 * d + 3] = kappa_of(label, rk, regions)
    waits[2].wait()
    for side, (wide, narrow) in enumerate(((wlo, nlo), (whi, nhi))):
        for c in range(3):
            wide[flow + c] = all_vel[c, side * (les_x - 1)]
            narrow[flow + c, pl.ds(0, les_x), :] = all_vel[c, :, side * (span_y - 1), :]
            narrow[flow + c, pl.ds(les_x, span_x - les_x), :] = jnp.zeros((span_x - les_x, vel.shape[3]), F32)
    waits[3].wait()
    for side, (wide, narrow) in enumerate(((wlo, nlo), (whi, nhi))):
        for d in range(DEEP):
            x = span_x - DEEP + d if side else d
            y = span_y - 1 - d if side else d
            for c in range(8):
                wide[8 * d + c] = all_pot[c, x]
                narrow[8 * d + c] = all_pot[c, :, y, :]


def corner_kernel(span_x, nlo, nhi, clo, chi):
    flat = 8 * DEEP
    for side, ref in enumerate((nlo, nhi)):
        for out, x, beyond in ((clo, 0, 1), (chi, span_x - 1, span_x - 2)):
            out[pl.ds(32 * side, 16), :] = ref[:16, x, :]
            out[pl.ds(32 * side + 16, 8), :] = ref[:8, beyond, :]
            out[pl.ds(32 * side + 24, 8), :] = ref[flat : flat + 8, x, :]


def corner_row(side, c, d, e):
    return 32 * side + (24 + c - 8 if c >= 8 else 8 * d + c if e == 0 else 16 + c)


def place(c, d):
    return 8 * d + c if c < 8 else 8 * DEEP + 4 * d + c - 8


def at(x):
    return (x + DEEP) * ROWS + OFF


def scale_plane(span_x, span_y, flags, field, x):
    line = lax.broadcasted_iota(jnp.int32, (8, field.shape[-1]), 0)
    fx = jnp.where(x < 0, flags[0], jnp.where(x >= span_x, flags[1], 1.0))
    for t in range(5):
        row = at(x) - FLAT + 8 * t
        y = line + (8 * t - FLAT)
        fy = jnp.where(y < 0, flags[2], jnp.where(y >= span_y, flags[3], 1.0))
        kappa = field[3, pl.ds(row, 8), :]
        field[4, pl.ds(row, 8), :] = (fx * fy) / (36.0 + kappa * kappa)


def sweep_plane(old, new, field, x, margin):
    for t in range(5):
        sweep_tile(old, new, field, at(x) - margin + 8 * t)


def over(low, high, do, unroll=1):
    def step(i, carry):
        do(i + low)
        return carry

    lax.fori_loop(0, high - low, step, 0, unroll=unroll)


def lanes(value):
    depth = value.shape[-1]
    lane = lax.broadcasted_iota(jnp.int32, value.shape, 1)
    ahead = jnp.where(lane == depth - 1, 0.0, pltpu.roll(value, depth - 1, 1))
    back = jnp.where(lane == 0, 0.0, pltpu.roll(value, 1, 1))
    return ahead, back


def sweep_tile(old, new, field, row):
    s6 = 6.0 * field[4, pl.ds(row, 8), :]
    kappa = field[3, pl.ds(row, 8), :]
    sk = kappa * field[4, pl.ds(row, 8), :]
    half = 0.5 * kappa
    total = []
    diff = []
    for c in range(8):
        xf = old[c, pl.ds(row + ROWS, 8), :]
        xb = old[c, pl.ds(row - ROWS, 8), :]
        yf = old[c, pl.ds(row + 1, 8), :]
        yb = old[c, pl.ds(row - 1, 8), :]
        zf, zb = lanes(old[c, pl.ds(row, 8), :])
        total.append((xf + xb) + (yf + yb) + (zf + zb))
        if c % 4 == 3:
            diff.append((xf - xb, yf - yb, zf - zb))
        else:
            diff.append(((xf - xb), (yf - yb), (zf - zb))[c % 4])
    for c in range(3):
        first = (field[c, pl.ds(row, 8), :] + total[c]) + half * diff[7][c]
        second = total[4 + c] - half * diff[3][c]
        new[c, pl.ds(row, 8), :] = s6 * first + sk * second
        new[4 + c, pl.ds(row, 8), :] = s6 * second - sk * first
    first = total[3] + half * (diff[4] + diff[5] + diff[6])
    second = total[7] - half * (diff[0] + diff[1] + diff[2])
    new[3, pl.ds(row, 8), :] = s6 * first + sk * second
    new[7, pl.ds(row, 8), :] = s6 * second - sk * first


def lorentz_tile(now, field, row):
    def grab(c, shift):
        return now[c, pl.ds(row + shift, 8), :]

    kappa = field[3, pl.ds(row, 8), :]

    def part(base):
        a = [grab(base + c, 0) for c in range(3)]
        azf, azb = lanes(a[0])
        bzf, bzb = lanes(a[1])
        curl = [
            (grab(base + 2, 1) - grab(base + 2, -1)) - (bzf - bzb),
            (azf - azb) - (grab(base + 2, ROWS) - grab(base + 2, -ROWS)),
            (grab(base + 1, ROWS) - grab(base + 1, -ROWS)) - (grab(base, 1) - grab(base, -1)),
        ]
        phi = grab(base + 3, 0)
        pzf, pzb = lanes(phi)
        grad = [
            grab(base + 3, ROWS) - grab(base + 3, -ROWS),
            grab(base + 3, 1) - grab(base + 3, -1),
            pzf - pzb,
        ]
        return curl, [a[c] + 0.5 * grad[c] for c in range(3)]

    real_b, field_re = part(0)
    imag_b, field_im = part(4)
    cur_re = [field[c, pl.ds(row, 8), :] + kappa * field_im[c] for c in range(3)]
    cur_im = [-kappa * field_re[c] for c in range(3)]
    force = []
    for c in range(3):
        n = (c + 1) % 3
        f = (c + 2) % 3
        value = (cur_re[n] * real_b[f] - cur_re[f] * real_b[n]) + (
            cur_im[n] * imag_b[f] - cur_im[f] * imag_b[n]
        )
        force.append(jnp.where(kappa > 0.0, 0.25 * value, 0.0))
    return force


def force_plane(now, field, force, span_y, x):
    for t in range(span_y // 8):
        f = lorentz_tile(now, field, at(x) + 8 * t)
        rows = pl.ds(pl.multiple_of(x * span_y + 8 * t, 8), 8)
        for c in range(3):
            force[c, rows, :] = f[c]


def stored(x):
    return pl.ds((x + DEEP) * ROWS, ROWS + OFF)


def kept(i):
    return pl.ds(i * (ROWS + OFF), ROWS + OFF)


def inner_kernel(
    span_x, span_y, regions, flags, rk, pot, src, lab, nlo, nhi,
    nxt, halves, nexts, fields, force, s0, s1, s2, field, some, tags, sems,
):
    copies = Copies(sems)
    early = [copies.start(lab, tags), copies.start(src, some)]
    late = [
        copies.start(pot.at[:, x], s0.at[:, pl.ds(at(x), span_y), :]) for x in range(span_x)
    ]
    for c in range(12):
        deep = DEEP if c < 8 else FLAT
        ref, part = (s0, c) if c < 8 else (field, c - 8)
        for d in range(deep):
            ref[part, strip(at(0) - 1 - d, span_x, ROWS), :] = nlo[place(c, d)] * flags[2]
            ref[part, strip(at(0) + span_y + d, span_x, ROWS), :] = nhi[place(c, d)] * flags[3]
    for one in early:
        one.wait()

    def lay(x):
        there = pl.ds(pl.multiple_of((x + DEEP) * ROWS + OFF, 8), span_y)
        label = tags[x]
        for c in range(3):
            field[c, there, :] = jnp.where(label < regions, some[c, x], 0.0)
        field[3, there, :] = kappa_of(label, rk, regions)

    over(0, span_x, lay)
    over(0, span_x, lambda x: scale_plane(span_x, span_y, flags, field, x))
    for one in late:
        one.wait()
    over(1, span_x - 1, lambda x: sweep_plane(s0, s1, field, x, 2), 7)
    over(2, span_x - 2, lambda x: sweep_plane(s1, s2, field, x, 1), 7)
    done = [
        copies.start(s2.at[:, pl.ds(at(x), span_y), :], nxt.at[:, x]) for x in range(2, span_x - 2)
    ]
    over(3, span_x - 3, lambda x: force_plane(s2, field, force, span_y, x), 5)
    for c in range(8):
        for i, x in enumerate((1, 2, span_x - 3, span_x - 2)):
            halves[c, kept(i), :] = s1[c, stored(x), :]
        for i, x in enumerate((2, 3, span_x - 4, span_x - 3)):
            nexts[c, kept(i), :] = s2[c, stored(x), :]
    for c in range(5):
        for i, x in enumerate((0, 1, 2, span_x - 3, span_x - 2, span_x - 1)):
            fields[c, kept(i), :] = field[c, stored(x), :]
    for one in done:
        one.wait()


def outer_kernel(
    span_x, span_y, slots, flags, pot, wlo, whi, nlo, nhi, clo, chi, hot_far, halves, nexts, fields, some_force, old_nxt,
    nxt, out, s0, s1, s2, field, force, sent, hot, sems, sent_sems,
):
    depth = pot.shape[-1]
    planes = 8 * DEEP + 4 * FLAT
    copies = Copies(sems)
    early = []
    late = []
    for d in range(FLAT):
        for ref, x in ((wlo, d - FLAT), (whi, span_x + d)):
            early.append(
                copies.start(ref.at[pl.ds(8 * DEEP + 4 * d, 4)], field.at[pl.ds(0, 4), pl.ds(at(x), span_y), :])
            )
    for d in range(DEEP):
        for ref, x in ((wlo, d - DEEP), (whi, span_x + d)):
            late.append(copies.start(ref.at[pl.ds(8 * d, 8)], s0.at[:, pl.ds(at(x), span_y), :]))
    for x in (0, 1, span_x - 2, span_x - 1):
        late.append(copies.start(pot.at[:, x], s0.at[:, pl.ds(at(x), span_y), :]))
    picks = copies.start(hot_far, hot)
    for c in range(8):
        for i, x in enumerate((1, 2, span_x - 3, span_x - 2)):
            s1[c, stored(x), :] = halves[c, kept(i), :]
        for i, x in enumerate((2, 3, span_x - 4, span_x - 3)):
            s2[c, stored(x), :] = nexts[c, kept(i), :]
    for c in range(3):
        rows = pl.ds(3 * span_y, (span_x - 6) * span_y)
        force[c, rows, :] = some_force[c, rows, :]
    for c in range(8):
        for d in range(DEEP):
            p = place(c, d)
            for x in (0, 1, span_x - 2, span_x - 1):
                s0[c, pl.ds(at(x) - 1 - d, 1), :] = nlo[p, pl.ds(x, 1), :] * flags[2]
                s0[c, pl.ds(at(x) + span_y + d, 1), :] = nhi[p, pl.ds(x, 1), :] * flags[3]
    for one in early:
        one.wait()
    for c in range(5):
        for i, x in enumerate((0, 1, 2, span_x - 3, span_x - 2, span_x - 1)):
            field[c, pl.ds(at(x) - 3, span_y + 6), :] = fields[c, pl.ds(i * (ROWS + OFF) + OFF - 3, span_y + 6), :]
    for c in range(12):
        deep = DEEP if c < 8 else FLAT
        ref, part = (s0, c) if c < 8 else (field, c - 8)
        for d in range(deep - 1):
            for e in range(deep - 1 - d):
                p = place(c, d)
                for source, x in ((clo, -1 - e), (chi, span_x + e)):
                    low, high = (source[pl.ds(corner_row(side, c, d, e), 1), :] for side in range(2))
                    ref[part, pl.ds(at(x) - 1 - d, 1), :] = low * flags[2]
                    ref[part, pl.ds(at(x) + span_y + d, 1), :] = high * flags[3]

    def both(low, high, do):
        over(-high, -low, do, 3)
        over(span_x + low, span_x + high, do, 3)

    both(0, 2, lambda x: scale_plane(span_x, span_y, flags, field, x))
    for one in late:
        one.wait()
    for i, first in enumerate((-DEEP, span_x)):

        @pl.when(flags[i] == 0.0)
        def _():
            for c in range(8):
                for x in range(first, first + DEEP):
                    s0[c, pl.ds(at(x) - DEEP, span_y + 2 * DEEP), :] = jnp.zeros((span_y + 2 * DEEP, depth), F32)

    both(-1, 2, lambda x: sweep_plane(s0, s1, field, x, 2))
    both(-2, 1, lambda x: sweep_plane(s1, s2, field, x, 1))
    done = [
        copies.start(s2.at[:, pl.ds(at(x), span_y), :], nxt.at[:, x])
        for x in (0, 1, span_x - 2, span_x - 1)
    ]
    both(-3, 0, lambda x: force_plane(s2, field, force, span_y, x))

    picks.wait()
    table = jnp.concatenate([force[c].astype(BF16) for c in range(3)], axis=1)
    chunk = 256
    upper = lax.broadcasted_iota(jnp.int32, (chunk // 8, 8, depth), 1) < slots
    for i in range(hot.shape[0] // chunk):
        h = hot[pl.ds(i * chunk, chunk), :]
        picked = jnp.dot(h, table, preferred_element_type=F32)
        got = [
            picked[:, c * depth : (c + 1) * depth].reshape(chunk // 8, 8, depth) for c in range(3)
        ]
        both_parts = jnp.concatenate([jnp.where(upper, got[0], got[1]), got[2]], axis=1)
        rows = pl.ds(i * (chunk // 8), chunk // 8)
        sent[rows] = both_parts.astype(BF16)
        one = pltpu.make_async_copy(sent.at[rows], out.at[rows], sent_sems.at[i])
        one.start()
        done.append(one)
    for one in done:
        one.wait()


def flow_kernel(les_x, span_y, flags, vel, wlo, whi, nlo, nhi, base, s0):
    first = 8 * DEEP + 4 * FLAT
    for c in range(3):
        for x in range(les_x):
            s0[c, pl.ds((x + 1) * ROWS + OFF, span_y), :] = vel[c, pl.ds(x * span_y, span_y), :]
        s0[c, pl.ds(OFF, span_y), :] = wlo[first + c] * flags[0]
        s0[c, pl.ds((les_x + 1) * ROWS + OFF, span_y), :] = whi[first + c] * flags[1]
        s0[c, strip(ROWS + OFF - 1, les_x, ROWS), :] = nlo[first + c, pl.ds(0, les_x), :] * flags[2]
        s0[c, strip(ROWS + OFF + span_y, les_x, ROWS), :] = nhi[first + c, pl.ds(0, les_x), :] * flags[3]

    def step(x, carry):
        for t in range(span_y // 8):
            row = (x + 1) * ROWS + OFF + 8 * t
            middle = [s0[c, pl.ds(row, 8), :] for c in range(3)]
            for c in range(3):
                xf = s0[c, pl.ds(row + ROWS, 8), :]
                xb = s0[c, pl.ds(row - ROWS, 8), :]
                yf = s0[c, pl.ds(row + 1, 8), :]
                yb = s0[c, pl.ds(row - 1, 8), :]
                zf, zb = lanes(middle[c])
                carried = 0.5 * (middle[0] * (xf - xb) + middle[1] * (yf - yb) + middle[2] * (zf - zb))
                spread = (xf + xb) + (yf + yb) + (zf + zb) - 6.0 * middle[c]
                base[c, pl.ds(pl.multiple_of(x * span_y + 8 * t, 8), 8), :] = middle[c] + DT * (
                    VISC * spread - carried
                )
        return carry

    lax.fori_loop(0, les_x, step, 0)


def last_kernel(slots, column, got, base, les, nxt):
    lines = base.shape[1]
    depth = got.shape[2]
    wide = got[...].astype(F32)
    values = jnp.concatenate(
        [wide[:, 8 * h : 8 * h + 8, :].reshape(-1, depth).astype(BF16) for h in range(2)], axis=1
    )
    want = column[...]
    lane = lax.broadcasted_iota(jnp.int32, want.shape, 1)
    take = jnp.concatenate(
        [
            jnp.concatenate(
                [
                    jnp.where(want == lane + (depth * k - slots * half), 1.0, 0.0).astype(BF16)
                    for k in range(values.shape[0] // depth)
                ],
                axis=1,
            )
            for half in range(2)
        ],
        axis=0,
    )
    picked = jnp.dot(take, values, preferred_element_type=F32)
    for c in range(3):
        part = picked[(c % 2) * lines : (c % 2 + 1) * lines, (c // 2) * depth : (c // 2 + 1) * depth]
        push = part.astype(BF16)
        les[c] = push
        nxt[c] = base[c] + DT * push.astype(F32)


def call(kernel, out, name, scratch=(), smem=0, count=1, hbm=(), hbm_out=(), alias=None, limit=16):
    vmem = pl.BlockSpec(memory_space=pltpu.VMEM)
    specs = [pl.BlockSpec(memory_space=pltpu.SMEM)] * smem + [vmem] * (count - smem)
    for i in hbm:
        specs[i] = pl.BlockSpec(memory_space=pltpu.HBM)
    return pl.pallas_call(
        kernel,
        out_shape=[jax.ShapeDtypeStruct(shape, kind) for shape, kind in out],
        in_specs=specs,
        out_specs=[
            pl.BlockSpec(memory_space=pltpu.HBM) if i in hbm_out else vmem for i in range(len(out))
        ],
        scratch_shapes=[pltpu.VMEM(*one) if isinstance(one, tuple) else one for one in scratch],
        input_output_aliases=alias or {},
        compiler_params=pltpu.CompilerParams(vmem_limit_bytes=limit * MIB),
        name=name,
    )


def swap(low, high, axis):
    count = lax.axis_size(axis)
    forward = [(i, (i + 1) % count) for i in range(count)]
    backward = [(target, source) for source, target in forward]
    return lax.ppermute(high, axis, forward), lax.ppermute(low, axis, backward)


def body(potential, source_current, cell_label, region_kappa, send_lines, recv_slot, velocity):
    _, span_x, span_y, depth = potential.shape
    les_x = velocity.shape[1]
    peers, slots = send_lines.shape[1:]
    regions = region_kappa.shape[0]
    cells = span_x * span_y
    lines = les_x * span_y
    planes = planes_of()
    vel = velocity.reshape(3, lines, depth)

    wide = ((planes, span_y, depth), F32)
    narrow = ((planes, span_x, depth), F32)
    wlo, whi, nlo, nhi = call(
        functools.partial(faces_kernel, span_x, span_y, regions),
        [wide, wide, narrow, narrow],
        "faces",
        scratch=[
            (potential.shape, F32),
            (source_current.shape, F32),
            (cell_label.shape, jnp.int32),
            (velocity.shape, F32),
            pltpu.SemaphoreType.DMA((4,)),
        ],
        smem=1, count=5, hbm=(1, 2, 3, 4), limit=60,
    )(region_kappa, potential, source_current, cell_label, velocity)
    nlo, nhi = swap(nlo, nhi, "narrow")
    wlo, whi = swap(wlo, whi, "wide")

    corner = ((64, depth), F32)
    clo, chi = call(
        functools.partial(corner_kernel, span_x), [corner, corner], "corner", count=2
    )(nlo, nhi)
    clo, chi = swap(clo, chi, "wide")

    pad = (span_x + 2 * DEEP) * ROWS + OFF
    padded = ((8, pad, depth), F32)
    fields = ((5, pad, depth), F32)
    w, n = lax.axis_index("wide"), lax.axis_index("narrow")
    flags = jnp.stack(
        [w > 0, w < lax.axis_size("wide") - 1, n > 0, n < lax.axis_size("narrow") - 1]
    ).astype(F32)
    keep = ROWS + OFF
    nxt, halves, nexts, edge_fields, force = call(
        functools.partial(inner_kernel, span_x, span_y, regions),
        [
            (potential.shape, F32),
            ((8, 4 * keep, depth), F32),
            ((8, 4 * keep, depth), F32),
            ((5, 6 * keep, depth), F32),
            ((3, cells, depth), F32),
        ],
        "inner",
        scratch=[
            padded,
            padded,
            padded,
            fields,
            ((3, span_x, span_y, depth), F32),
            ((span_x, span_y, depth), jnp.int32),
            pltpu.SemaphoreType.DMA((2 + 2 * span_x,)),
        ],
        smem=2, count=7, hbm=(2, 3, 4), hbm_out=(0,), limit=LIMIT_IN,
    )(flags, region_kappa, potential, source_current, cell_label, nlo, nhi)

    sent = jnp.concatenate([send_lines[0], send_lines[0]], axis=1).reshape(-1)
    hot = (sent[:, None] == jnp.arange(cells, dtype=jnp.int32)[None, :]).astype(BF16)
    potential_next, outgoing = call(
        functools.partial(outer_kernel, span_x, span_y, slots),
        [(potential.shape, F32), ((peers, 16, depth), BF16)],
        "outer",
        scratch=[
            padded,
            padded,
            padded,
            fields,
            ((3, cells, depth), F32),
            ((peers, 16, depth), BF16),
            (hot.shape, BF16),
            pltpu.SemaphoreType.DMA((2 * FLAT + 2 * DEEP + 9,)),
            pltpu.SemaphoreType.DMA((hot.shape[0] // 256,)),
        ],
        smem=1, count=14, hbm=(1, 2, 3, 8, 13), hbm_out=(0, 1), alias={13: 0}, limit=LIMIT_OUT,
    )(flags, potential, wlo, whi, nlo, nhi, clo, chi, hot, halves, nexts, edge_fields, force, nxt)

    incoming = lax.all_to_all(
        outgoing, ("wide", "narrow"), split_axis=0, concat_axis=0, tiled=True
    )
    slot = recv_slot[0]
    column = jnp.broadcast_to(((slot // slots) * 8 + slot % slots)[:, None], (lines, 128))
    (base,) = call(
        functools.partial(flow_kernel, les_x, span_y),
        [((3, lines, depth), F32)],
        "flow",
        scratch=[((3, (les_x + 2) * ROWS + OFF, depth), F32)],
        smem=1, count=6,
    )(flags, vel, wlo, whi, nlo, nhi)
    les, velocity_next = call(
        functools.partial(last_kernel, slots),
        [((3, lines, depth), BF16), ((3, lines, depth), F32)],
        "last", count=3,
    )(column, incoming, base)
    block = (3, les_x, span_y, depth)
    return potential_next, les.reshape(block), velocity_next.reshape(block)


def solution(mesh):
    in_specs = (
        P(None, "wide", "narrow", None),
        P(None, "wide", "narrow", None),
        P("wide", "narrow", None),
        P(),
        P(("wide", "narrow"), None, None),
        P(("wide", "narrow"), None),
        P(None, "wide", "narrow", None),
    )
    out_specs = (
        P(None, "wide", "narrow", None),
        P(None, "wide", "narrow", None),
        P(None, "wide", "narrow", None),
    )
    return jax.shard_map(body, mesh=mesh, in_specs=in_specs, out_specs=out_specs, check_vma=False)
```
